512 devices in a mesh: dp: 128 (over y_lo, x, z), mp: 4 (over y_hi, core).
Axes of the slice: x: 4, y: 8 (y_hi: 2, y_lo: 4; y = y_hi * 4 + y_lo), z: 8, core: 2. Of those that a mesh axis runs over, the one named last changes fastest.
Arguments:
- features: bfloat16 [16384, 1536], P('dp', 'mp'), may hold values from -240 to 240
- proj_weight: bfloat16 [1536, 1152], P('mp'), may hold values from -0.15625 to 0.15625
- texts: bfloat16 [16384, 1152], P(('dp', 'mp')), may hold values from -6 to 6
Outputs:
- grad_features: bfloat16 [16384, 1536], P('dp', 'mp')
- grad_weight: float32 [1536, 1152], P('mp')
The draws below stay inside these ranges and needn't reach their ends.
All inputs are finite; a program needn't handle non-finite values.
Results may differ from the reference program's by a relative error of at most 0.011.
Values may be sent and summed in bfloat16 or wider, within the bound.
A program may use at most 64 MiB of HBM per device.

```python
import math
import jax
import jax.numpy as jnp
from jax import lax

W = 1536
E = 1152
BATCH = 16384


def draw_features(key, part):
    key = jax.random.fold_in(key, 11)
    key_base, key_cols, key_rows = jax.random.split(key, 3)
    columns = jnp.arange(W, dtype=jnp.float32) / (W - 1)
    col_scale = 3.0 ** columns * jax.random.uniform(key_cols, (W,), jnp.float32, 0.7, 1.4)
    row_scale = jnp.exp(jax.random.uniform(key_rows, (BATCH, 1), jnp.float32, 0.0, math.log(10.0)))
    base = jnp.clip(jax.random.normal(key_base, (BATCH, W), jnp.float32), -4.0, 4.0)
    values = base * col_scale[None, :] * row_scale
    return values.astype(jnp.bfloat16)


def block_levels(key, shape, pieces, smallest, top_value):
    gain = 1.0
    for axis_at, blocks in pieces:
        heights = jax.random.uniform(jax.random.fold_in(jax.random.fold_in(key, 6), axis_at), (blocks,), jnp.float32, smallest / len(pieces), top_value / len(pieces))
        gain = gain * jnp.repeat(jnp.exp(heights), shape[axis_at] // blocks).reshape((-1,) + (1,) * (len(shape) - 1 - axis_at))
    return gain


def normal_values(key, dims, scale, limit, cuts=(), kind=jnp.bfloat16):
    level = block_levels(key, dims, cuts, -0.22, 0.18) if cuts else 1.0
    entries = jax.random.normal(key, dims, jnp.float32) * scale * level
    return jnp.minimum(jnp.maximum(entries, -limit), limit).astype(kind)


def setup_inputs(seed: int = 0) -> dict:
    keys = jax.random.split(jax.random.key(seed), 4)
    features = draw_features(jax.random.fold_in(keys[3], 71), 0)
    proj_weight = normal_values(keys[1], (W, E), W ** -0.5, 0.15625, ((0, 4),))
    texts = normal_values(keys[2], (BATCH, E), 1.0, 6.0, ((0, 512),))
    return dict(features=features, proj_weight=proj_weight, texts=texts)


logit_scale = 100.0
logit_bias = -10.0
epsilon = 1e-06

def unit_rows(values):
    return values * lax.rsqrt(lax.optimization_barrier(jnp.sum(values * values, axis=1, keepdims=True)) + epsilon)

def reference(features, proj_weight, texts):
    inputs = features.astype(jnp.float32)
    mean_in = lax.optimization_barrier(jnp.mean(inputs, axis=1, keepdims=True))
    centred = inputs - mean_in
    normed_b = centred.astype(jnp.bfloat16)
    project = jnp.dot(normed_b, proj_weight, preferred_element_type=jnp.float32)
    inv_norm = lax.rsqrt(lax.optimization_barrier(jnp.sum(project * project, axis=1, keepdims=True)) + epsilon)
    unit_img = project * inv_norm
    unit_img_b = unit_img.astype(jnp.bfloat16)
    unit_txt_b = unit_rows(texts.astype(jnp.float32)).astype(jnp.bfloat16)
    total = unit_txt_b.shape[0]
    text_ids = jnp.arange(total, dtype=jnp.int32)
    block = math.gcd(total, 512)

    def one_block(pair):
        rows_b, row_ids = pair
        logits = logit_scale * jnp.dot(rows_b, unit_txt_b.T, preferred_element_type=jnp.float32) + logit_bias
        labels = jnp.where(row_ids[:, None] == text_ids[None, :], 1.0, -1.0).astype(jnp.float32)
        slopes = (-labels * jax.nn.sigmoid(-labels * logits)).astype(jnp.bfloat16)
        return logit_scale * jnp.dot(slopes, unit_txt_b, preferred_element_type=jnp.float32)
    grad_unit = lax.map(one_block, (unit_img_b.reshape(total // block, block, -1), text_ids.reshape(total // block, block)))
    grad_unit = grad_unit.reshape(total, -1)
    grad_proj = inv_norm * (grad_unit - unit_img * lax.optimization_barrier(jnp.sum(unit_img * grad_unit, axis=1, keepdims=True)))
    grad_proj_b = grad_proj.astype(jnp.bfloat16)
    grad_weight = jnp.dot(normed_b.T, grad_proj_b, preferred_element_type=jnp.float32)
    grad_normed = jnp.dot(grad_proj_b, proj_weight.T, preferred_element_type=jnp.float32)
    grad_mean = lax.optimization_barrier(jnp.mean(grad_normed, axis=1, keepdims=True))
    grad_in = grad_normed - grad_mean
    return (grad_in.astype(jnp.bfloat16), grad_weight)
```

```python
import jax
import jax.numpy as jnp
from jax import lax
from jax.experimental import pallas as pl
from jax.experimental.pallas import tpu as pltpu
from jax.sharding import PartitionSpec as P

logit_scale = 100.0
logit_bias = -10.0
epsilon = 1e-06
NX, NYL, NZ = 4, 4, 8
NY = 2 * NYL
MESH = pl.DeviceIdType.MESH
NT = (((1,), (1,)), ((), ()))


def place(x, y, z, c):
    return ((y % NYL) * NX + x) * NZ + z, (y // NYL) * 2 + c


def unit_scale(values):
    return lax.rsqrt(jnp.sum(values * values, axis=1, keepdims=True) + epsilon)


def tile_slots():
    slots = []
    for i in range(6):
        for j in range(9):
            q = i * 9 + j
            slots.append((i, j, q % NX, (q // NX) % NZ, q // (NX * NZ)))
    return slots


def kernel(
    feat_ref, w_ref, text_ref, gfeat_ref, gweight_ref,
    txt, sums, cols, normed, nt_send, nt, part, part_core, part_far, unit, img,
    grad, grad_core, half_send, half_recv, gproj, wsend, wx, zsend, wz, fin,
    tx_s, tx_r, tz_s, tz_r, su_s, su_r, co_s, co_r, nt_s, nt_r, pc_s, pc_r, im_s, im_r,
    gc_s, gc_r, gy_s, gy_r, gp_s, gp_r, wx_s, wx_r, wz_s, wz_r, fy_s, fy_r, fz_s, fz_r, fx_s, fx_r,
):
    dp = lax.axis_index("dp")
    mp = lax.axis_index("mp")
    yl = dp // (NX * NZ)
    x = (dp // NZ) % NX
    z = dp % NZ
    yh = mp // 2
    c = mp % 2
    y = yh * NYL + yl
    sib = place(x, y, z, 1 - c)
    y_far = (y + NYL) % NY
    far = place(x, y_far, z, c)
    far_sib = place(x, y_far, z, 1 - c)

    def on_y(k):
        return place(x, (y + k) % NY, z, c)

    def on_yl(k):
        return place(x, yh * NYL + (yl + k) % NYL, z, c)

    def on_x(k):
        return place((x + k) % NX, y, z, c)

    def on_z(k):
        return place(x, y, (z + k) % NZ, c)

    def send(src, dst, s, r, to):
        copy = pltpu.make_async_remote_copy(
            src_ref=src, dst_ref=dst, send_sem=s, recv_sem=r, device_id=to, device_id_type=MESH
        )
        copy.start()
        return copy

    barrier = pltpu.get_barrier_semaphore()
    others = [sib, far_sib]
    others += [on_y(k) for k in range(1, NY)]
    others += [on_x(k) for k in range(1, NX)]
    others += [on_z(k) for k in range(1, NZ)]
    for other in others:
        pl.semaphore_signal(barrier, inc=1, device_id=other, device_id_type=MESH)

    text = text_ref[...].astype(jnp.float32)
    txt[z, x] = (text * unit_scale(text)).astype(jnp.bfloat16)
    inputs = feat_ref[...].astype(jnp.float32)
    row_sum = jnp.sum(inputs, axis=1, keepdims=True)
    sums[mp] = jnp.broadcast_to(row_sum, (128, 128)).T[:8]
    weights = w_ref[...]
    cols[mp] = jnp.broadcast_to(
        jnp.sum(weights.astype(jnp.float32), axis=0, keepdims=True), (8, weights.shape[1])
    )
    pl.semaphore_wait(barrier, len(others))

    mates = [sib, far, far_sib]
    sum_copies = [send(sums.at[mp], sums.at[mp], su_s.at[k], su_r.at[k], to) for k, to in enumerate(mates)]
    text_copies = [
        send(txt.at[z, x], txt.at[z, x], tx_s.at[k - 1], tx_r.at[k - 1], on_x(k)) for k in range(1, NX)
    ]
    col_copies = [send(cols.at[mp], cols.at[mp], co_s.at[k], co_r.at[k], to) for k, to in enumerate(mates)]

    def text_step(step, before):
        for copy in before:
            copy.wait()
        copies = []
        for way, d in enumerate((1, -1)):
            slot = (z - d * (step - 1) + 2 * NZ) % NZ
            block = txt.at[slot]
            if step == NZ // 2:
                block = txt.at[slot, pl.ds(way * (NX // 2), NX // 2)]
            index = (step - 1) * 2 + way
            copies.append(send(block, block, tz_s.at[index], tz_r.at[index], on_z((d + NZ) % NZ)))
        return copies

    for copy in sum_copies:
        copy.wait()
    total = (sums[0] + sums[1]) + (sums[2] + sums[3])
    mean_in = jnp.broadcast_to(total[:1] / 1536.0, (128, 128)).T[:, :1]
    centred = inputs - mean_in
    normed[...] = centred.astype(jnp.bfloat16)
    ring = text_step(1, text_copies)
    partial = jnp.dot(normed[...], weights, preferred_element_type=jnp.float32)
    for h in range(2):
        for b in range(2):
            part[b, h] = partial[(h * 2 + b) * 32 : (h * 2 + b + 1) * 32]
    core_copy = send(part.at[1 - c], part_core, pc_s.at[0], pc_r.at[0], sib)
    turned = centred.T.astype(jnp.bfloat16)
    for g in range(NYL):
        nt_send[g] = turned[g * 96 : (g + 1) * 96]
    nt[yl] = nt_send[yl]
    core_copy.wait()
    part[c, 1 - yh] += part_core[1 - yh]
    far_copy = send(part.at[c, 1 - yh], part_far, pc_s.at[1], pc_r.at[1], far)
    nt_copies = [
        send(nt_send.at[(yl + k) % NYL], nt.at[yl], nt_s.at[k - 1], nt_r.at[k - 1], on_yl(k))
        for k in range(1, NYL)
    ]
    ring = text_step(2, ring)
    far_copy.wait()
    project = part[c, yh] + part_core[yh] + part_far[...]
    inv_norm = unit_scale(project)
    unit_img = project * inv_norm
    unit[...] = unit_img
    img[c, y] = unit_img.astype(jnp.bfloat16)
    img_copies = [
        send(img.at[c, y], img.at[c, y], im_s.at[k], im_r.at[k], on_y(k)) for k in range(1, NY)
    ]
    ring = text_step(3, ring)
    for copy in img_copies:
        copy.wait()
    img_core = send(img.at[c], img.at[c], im_s.at[0], im_r.at[0], sib)
    ring = text_step(4, ring)
    grad[...] = jnp.zeros_like(grad)
    img_core.wait()
    for copy in ring:
        copy.wait()

    @pl.loop(0, NZ // 2)
    def _(b):
        texts = txt[pl.ds(b * 2, 2)].reshape(2 * NX * 32, -1)
        images = img[...].reshape(2 * NY * 32, -1)
        score = lax.dot_general(images, texts, NT, preferred_element_type=jnp.float32)
        logits = logit_scale * score + logit_bias
        rows = lax.broadcasted_iota(jnp.int32, logits.shape, 0)
        columns = lax.broadcasted_iota(jnp.int32, logits.shape, 1) + b * (2 * NX * 32)
        same = rows - (c * NY + y) * 32 == columns - (z * NX + x) * 32
        own = (rows // 32) == (c * NY + y)
        same = jnp.logical_and(same, own)
        slope = jax.nn.sigmoid(jnp.where(same, -logits, logits))
        slope = jnp.where(same, -slope, slope).astype(jnp.bfloat16)
        grad[...] += jnp.dot(slope, texts, preferred_element_type=jnp.float32).reshape(grad.shape)

    grad_core_copy = send(grad.at[1 - c], grad_core, gc_s.at[0], gc_r.at[0], sib)
    grad_core_copy.wait()
    summed = grad[c] + grad_core[...]
    grad[c] = summed
    half_send[...] = summed.astype(jnp.bfloat16)
    half_copies = [
        send(half_send.at[(y + k) % NY], half_recv.at[y], gy_s.at[k - 1], gy_r.at[k - 1], on_y(k))
        for k in range(1, NY)
    ]
    half_recv[y] = jnp.zeros(half_recv.shape[1:], half_recv.dtype)
    grad_unit = grad[c, y]
    for copy in half_copies:
        copy.wait()
    for k in range(NY):
        grad_unit = grad_unit + half_recv[k].astype(jnp.float32)
    grad_unit = logit_scale * grad_unit
    unit_img = unit[...]
    along = jnp.sum(unit_img * grad_unit, axis=1, keepdims=True)
    gproj[c, y] = (inv_norm * (grad_unit - unit_img * along)).astype(jnp.bfloat16)
    gp_copies = [
        send(gproj.at[c, y], gproj.at[c, y], gp_s.at[k], gp_r.at[k], on_y(k)) for k in range(1, NY)
    ]
    wsend[...] = jnp.zeros_like(wsend)
    for copy in col_copies + nt_copies:
        copy.wait()
    for copy in gp_copies:
        copy.wait()
    gp_core = send(gproj.at[c], gproj.at[c], gp_s.at[0], gp_r.at[0], sib)
    gp_core.wait()

    def group_rows(g):
        return jnp.concatenate([gproj[0, g], gproj[1, g], gproj[0, g + NYL], gproj[1, g + NYL]], axis=0)

    weight_part = jnp.dot(nt[0], group_rows(0), preferred_element_type=jnp.float32)
    for g in range(1, NYL):
        weight_part += jnp.dot(nt[g], group_rows(g), preferred_element_type=jnp.float32)
    weight_part = weight_part.astype(jnp.bfloat16)
    slots = tile_slots()
    for i, j, tx, tz, k in slots:
        wsend[tx, tz, k] = weight_part[i * 16 : (i + 1) * 16, j * 128 : (j + 1) * 128]
    wx_copies = [
        send(wsend.at[(x + k) % NX], wx.at[x], wx_s.at[k - 1], wx_r.at[k - 1], on_x(k)) for k in range(1, NX)
    ]
    rows = group_rows(yl)
    grad_normed = lax.dot_general(rows, weights, NT, preferred_element_type=jnp.float32)
    col = (cols[0] + cols[1]) + (cols[2] + cols[3])
    grad_total = jnp.sum(rows.astype(jnp.float32) * col[:1], axis=1, keepdims=True)
    gfeat_ref[...] = (grad_normed - grad_total / 1536.0).astype(jnp.bfloat16)
    wx[x] = wsend[x]
    for copy in wx_copies:
        copy.wait()
    over_x = wx[0].astype(jnp.float32)
    for k in range(1, NX):
        over_x += wx[k].astype(jnp.float32)
    zsend[...] = over_x.astype(jnp.bfloat16)
    wz_copies = [
        send(zsend.at[(z + k) % NZ], wz.at[z], wz_s.at[k - 1], wz_r.at[k - 1], on_z(k)) for k in range(1, NZ)
    ]
    wz[z] = zsend[z]
    for copy in wz_copies:
        copy.wait()
    over_z = wz[0].astype(jnp.float32)
    for k in range(1, NZ):
        over_z += wz[k].astype(jnp.float32)
    fin[x, z, yl] = over_z.astype(jnp.bfloat16)
    for copy in [
        send(fin.at[x, z, yl], fin.at[x, z, yl], fy_s.at[k - 1], fy_r.at[k - 1], on_yl(k))
        for k in range(1, NYL)
    ]:
        copy.wait()
    for copy in [
        send(fin.at[x, z], fin.at[x, z], fz_s.at[k - 1], fz_r.at[k - 1], on_z(k)) for k in range(1, NZ)
    ]:
        copy.wait()
    for copy in [send(fin.at[x], fin.at[x], fx_s.at[k - 1], fx_r.at[k - 1], on_x(k)) for k in range(1, NX)]:
        copy.wait()
    for g in range(NYL):
        for i, j, tx, tz, k in slots:
            gweight_ref[g * 96 + i * 16 : g * 96 + (i + 1) * 16, j * 128 : (j + 1) * 128] = fin[tx, tz, g, k]


def shards(features, proj_weight, texts):
    rows, width = features.shape
    e = proj_weight.shape[1]
    bf16, f32 = jnp.bfloat16, jnp.float32
    dma = pltpu.SemaphoreType.DMA
    counts = [NX - 1, NZ, 3, 3, NYL - 1, 2, NY, 1, NY - 1, NY, NX - 1, NZ - 1, NYL - 1, NZ - 1, NX - 1]
    semaphores = [dma((n,)) for n in counts for _ in range(2)]
    grad_features, grad_weight = pl.pallas_call(
        kernel,
        out_shape=(
            jax.ShapeDtypeStruct((rows, width), bf16),
            jax.ShapeDtypeStruct((width, e), bf16),
        ),
        in_specs=[pl.BlockSpec(memory_space=pltpu.VMEM)] * 3,
        out_specs=[pl.BlockSpec(memory_space=pltpu.VMEM)] * 2,
        scratch_shapes=[
            pltpu.VMEM((NZ, NX, 32, e), bf16),
            pltpu.VMEM((4, 8, 128), f32),
            pltpu.VMEM((4, 8, e), f32),
            pltpu.VMEM((rows, width), bf16),
            pltpu.VMEM((NYL, width // NYL, rows), bf16),
            pltpu.VMEM((NYL, width // NYL, rows), bf16),
            pltpu.VMEM((2, 2, 32, e), f32),
            pltpu.VMEM((2, 32, e), f32),
            pltpu.VMEM((32, e), f32),
            pltpu.VMEM((32, e), f32),
            pltpu.VMEM((2, NY, 32, e), bf16),
            pltpu.VMEM((2, NY, 32, e), f32),
            pltpu.VMEM((NY, 32, e), f32),
            pltpu.VMEM((NY, 32, e), bf16),
            pltpu.VMEM((NY, 32, e), bf16),
            pltpu.VMEM((2, NY, 32, e), bf16),
            pltpu.VMEM((NX, NZ, 2, 16, 128), bf16),
            pltpu.VMEM((NX, NZ, 2, 16, 128), bf16),
            pltpu.VMEM((NZ, 2, 16, 128), bf16),
            pltpu.VMEM((NZ, 2, 16, 128), bf16),
            pltpu.VMEM((NX, NZ, NYL, 2, 16, 128), bf16),
        ]
        + semaphores,
        compiler_params=pltpu.CompilerParams(
            collective_id=0, has_side_effects=True, vmem_limit_bytes=48 << 20
        ),
        cost_estimate=pl.CostEstimate(flops=2_750_000_000, bytes_accessed=8_000_000, transcendentals=524288),
        name="head_loss",
    )(features, proj_weight, texts)
    return grad_features, grad_weight.astype(f32)


def solution(mesh):
    return jax.shard_map(
        shards,
        mesh=mesh,
        in_specs=(P("dp", "mp"), P("mp", None), P(("dp", "mp"), None)),
        out_specs=(P("dp", "mp"), P("mp", None)),
        check_vma=False,
    )
```

```python
import jax
import jax.numpy as jnp
from jax import lax
from jax.experimental import pallas as pl
from jax.experimental.pallas import tpu as pltpu
from jax.sharding import PartitionSpec as P

logit_scale = 100.0
logit_bias = -10.0
epsilon = 1e-06
NX, NYL, NZ = 4, 4, 8
NY = 2 * NYL
MESH = pl.DeviceIdType.MESH
NT = (((1,), (1,)), ((), ()))


def place(x, y, z, c):
    return ((y % NYL) * NX + x) * NZ + z, (y // NYL) * 2 + c


def unit_scale(values):
    return lax.rsqrt(jnp.sum(values * values, axis=1, keepdims=True) + epsilon)


def tile_slots():
    slots = []
    for i in range(6):
        for j in range(9):
            q = i * 9 + j
            slots.append((i, j, q % NX, (q // NX) % NZ, q // (NX * NZ)))
    return slots


def remote(src, dst, s, r, to):
    copy = pltpu.make_async_remote_copy(
        src_ref=src, dst_ref=dst, send_sem=s, recv_sem=r, device_id=to, device_id_type=MESH
    )
    copy.start()
    return copy


def wait_all(copies):
    for copy in copies:
        copy.wait()


def share(at, me, count, to, s, r):
    def go(index, k):
        return remote(at(me, None), at(me, None), s.at[index], r.at[index], to(k))

    return [go(0, 2), go(1, count - 2), go(2, 1), go(3, count - 1)]


def pass_on(at, me, count, to, s, r, copies):
    low = (me + count - 2) % count
    high = (me + 2) % count
    copies[0].wait_recv()
    on = [
        remote(at(low, None), at(low, None), s.at[4], r.at[4], to(1)),
        remote(at(low, 0), at(low, 0), s.at[5], r.at[5], to(2)),
    ]
    copies[1].wait_recv()
    on += [
        remote(at(high, None), at(high, None), s.at[6], r.at[6], to(count - 1)),
        remote(at(high, 1), at(high, 1), s.at[7], r.at[7], to(count - 2)),
    ]
    return on


def finish(copies, on):
    copies[0].wait_send()
    copies[1].wait_send()
    wait_all(copies[2:] + on)


def kernel(
    feat_hbm, w_hbm, text_hbm, gfeat_ref, gweight_ref,
    feat, w, text_in, txt, sums, cols, normed, nt_send, nt, part, part_core, part_far, unit, img,
    grad, gs, g_three, g_four, g_one, g_sum, g_two, gproj, wsend, wx, zsend, wz, fin_y, fin_a, fin_b,
    in_s, ax_s, ax_r, az_s, az_r, bx_s, bx_r, bz_s, bz_r, ts_s, ts_r,
    su_s, su_r, co_s, co_r, nt_s, nt_r, pc_s, pc_r, im_s, im_r,
    gy_s, gy_r, gp_s, gp_r, gc_s, gc_r, wx_s, wx_r, wz_s, wz_r, fy_s, fy_r,
    fax_s, fax_r, faz_s, faz_r, fbx_s, fbx_r, fbz_s, fbz_r,
):
    dp = lax.axis_index("dp")
    mp = lax.axis_index("mp")
    yl = dp // (NX * NZ)
    x = (dp // NZ) % NX
    z = dp % NZ
    yh = mp // 2
    c = mp % 2
    y = yh * NYL + yl
    sib = place(x, y, z, 1 - c)
    y_far = (y + NYL) % NY
    far = place(x, y_far, z, c)
    far_sib = place(x, y_far, z, 1 - c)

    def on_y(k):
        return place(x, (y + k) % NY, z, c)

    def on_yl(k):
        return place(x, yh * NYL + (yl + k) % NYL, z, c)

    def on_x(k):
        return place((x + k) % NX, y, z, c)

    def on_z(k):
        return place(x, y, (z + k) % NZ, c)

    barrier = pltpu.get_barrier_semaphore()
    others = [sib, far_sib]
    others += [on_y(k) for k in range(1, NY)]
    others += [on_x(k) for k in range(1, NX)]
    others += [on_z(k) for k in range(1, NZ)]
    for other in others:
        pl.semaphore_signal(barrier, inc=1, device_id=other, device_id_type=MESH)

    text_load = pltpu.make_async_copy(text_hbm, text_in, in_s.at[0])
    feat_load = pltpu.make_async_copy(feat_hbm, feat, in_s.at[1])
    w_load = pltpu.make_async_copy(w_hbm, w, in_s.at[2])
    feat_load.start()
    text_load.start()
    w_load.start()

    feat_load.wait()
    inputs = feat[...].astype(jnp.float32)
    row_sum = jnp.sum(inputs, axis=1, keepdims=True)
    sums[mp] = jnp.broadcast_to(row_sum, (128, 128)).T[:8]
    text_load.wait()
    text = text_in[...].astype(jnp.float32)
    own_text = (text * unit_scale(text)).astype(jnp.bfloat16)
    txt[c, 0, z * NX + x] = own_text[:16]
    txt[c, 1, x * NZ + z] = own_text[16:]
    pl.semaphore_wait(barrier, len(others))

    mates = [sib, far, far_sib]
    sum_copies = [remote(sums.at[mp], sums.at[mp], su_s.at[k], su_r.at[k], to) for k, to in enumerate(mates)]

    own_a = txt.at[c, 0, z * NX + x]
    a_x = [remote(own_a, own_a, ax_s.at[k - 1], ax_r.at[k - 1], on_x(k)) for k in range(1, NX)]

    def b_at(slot, half):
        block = txt.at[c, 1, x * NZ + slot]
        if half is None:
            return block
        return block.at[:, pl.ds(0, 640)] if half == 0 else block.at[:, pl.ds(640, 512)]

    def a_at(slot, half):
        if half is None:
            return txt.at[c, 0, pl.ds(slot * NX, NX)]
        return txt.at[c, 0, pl.ds(slot * NX + half * (NX // 2), NX // 2)]

    b_z = share(b_at, z, NZ, on_z, bz_s, bz_r)

    w_load.wait()
    weights = w[...]
    cols[mp] = jnp.broadcast_to(
        jnp.sum(weights.astype(jnp.float32), axis=0, keepdims=True), (8, weights.shape[1])
    )

    wait_all(sum_copies)
    total = (sums[0] + sums[1]) + (sums[2] + sums[3])
    mean_in = jnp.broadcast_to(total[:1] / 1536.0, (128, 128)).T[:, :1]
    centred = inputs - mean_in
    normed[...] = centred.astype(jnp.bfloat16)
    wait_all(a_x)
    a_z = share(a_at, z, NZ, on_z, az_s, az_r)
    partial = jnp.dot(normed[...], weights, preferred_element_type=jnp.float32)
    for h in range(2):
        for b in range(2):
            part[b, h] = partial[(h * 2 + b) * 32 : (h * 2 + b + 1) * 32]
    core_copy = remote(part.at[1 - c], part_core, pc_s.at[0], pc_r.at[0], sib)
    b_on = pass_on(b_at, z, NZ, on_z, bz_s, bz_r, b_z)
    core_copy.wait()
    part[c, 1 - yh] += part_core[1 - yh]
    far_copy = remote(part.at[c, 1 - yh], part_far, pc_s.at[1], pc_r.at[1], far)
    turned = centred.T.astype(jnp.bfloat16)
    for g in range(NYL):
        nt_send[g] = turned[g * 96 : (g + 1) * 96]
    nt[yl] = nt_send[yl]
    finish(b_z, b_on)
    own_b = txt.at[c, 1, pl.ds(x * NZ, NZ)]
    b_x = [remote(own_b, own_b, bx_s.at[k - 1], bx_r.at[k - 1], on_x(k)) for k in range(1, NX)]
    far_copy.wait()
    project = part[c, yh] + part_core[yh] + part_far[...]
    inv_norm = unit_scale(project)
    unit_img = project * inv_norm
    unit[...] = unit_img
    img[y] = unit_img.astype(jnp.bfloat16)

    def img_at(slot, half):
        return img.at[slot] if half is None else img.at[slot, pl.ds(half * 16, 16)]

    img_one = share(img_at, y, NY, on_y, im_s, im_r)
    col_copies = [remote(cols.at[mp], cols.at[mp], co_s.at[k], co_r.at[k], to) for k, to in enumerate(mates)]
    nt_copies = [
        remote(nt_send.at[(yl + k) % NYL], nt.at[yl], nt_s.at[k - 1], nt_r.at[k - 1], on_yl(k))
        for k in range(1, NYL)
    ]
    a_on = pass_on(a_at, z, NZ, on_z, az_s, az_r, a_z)
    img_on = pass_on(img_at, y, NY, on_y, im_s, im_r, img_one)
    wait_all(b_x)
    text_b = remote(txt.at[c, 1], txt.at[c, 1], ts_s.at[1], ts_r.at[1], sib)
    finish(a_z, a_on)
    text_a = remote(txt.at[c, 0], txt.at[c, 0], ts_s.at[0], ts_r.at[0], sib)
    grad[...] = jnp.zeros_like(grad)
    finish(img_one, img_on)

    def add_texts(core, way):
        texts = txt[core, way].reshape(NX * NZ * 16, -1)
        images = img[...].reshape(NY * 32, -1)
        score = lax.dot_general(images, texts, NT, preferred_element_type=jnp.float32)
        slope = jax.nn.sigmoid(logit_scale * score + logit_bias).astype(jnp.bfloat16)
        grad[...] += jnp.dot(slope, texts, preferred_element_type=jnp.float32).reshape(grad.shape)

    @pl.loop(0, 2)
    def _(way):
        add_texts(c, way)

    text_a.wait()
    text_b.wait()

    @pl.loop(0, 2)
    def _(way):
        add_texts(1 - c, way)

    for k in (3, 4, 5, 1, 7):
        gs[(y + k) % NY] = grad[(y + k) % NY].astype(jnp.bfloat16)

    def give(src, dst, index, k):
        return remote(src, dst, gy_s.at[index], gy_r.at[index], on_y(k))

    three = [
        give(gs.at[(y + 3) % NY], g_three.at[0], 0, 1),
        give(gs.at[(y + NY - 3) % NY], g_three.at[1], 1, NY - 1),
    ]
    four = [
        give(gs.at[(y + 4) % NY, pl.ds(0, 16)], g_four.at[0], 2, 2),
        give(gs.at[(y + 4) % NY, pl.ds(16, 16)], g_four.at[1], 3, NY - 2),
    ]
    one = [
        give(gs.at[(y + 1) % NY], g_one.at[0], 4, 1),
        give(gs.at[(y + NY - 1) % NY], g_one.at[1], 5, NY - 1),
    ]
    own_b16 = img[y].astype(jnp.float32)
    own_t = jnp.concatenate([txt[c, 0, z * NX + x], txt[c, 1, x * NZ + z]], axis=0).astype(jnp.float32)
    own_logit = logit_scale * jnp.sum(own_b16 * own_t, axis=1, keepdims=True) + logit_bias
    wrong = jax.nn.sigmoid(own_logit).astype(jnp.bfloat16).astype(jnp.float32)
    right = (-jax.nn.sigmoid(-own_logit)).astype(jnp.bfloat16).astype(jnp.float32)
    grad_unit = grad[y] + (right - wrong) * own_t
    wsend[...] = jnp.zeros_like(wsend)
    two = []
    for side, k in ((0, 2), (1, NY - 2)):
        three[side].wait()
        four[side].wait()
        far_sum = grad[(y + k) % NY] + g_three[side].astype(jnp.float32)
        lo, hi = far_sum[:16], far_sum[16:]
        if side == 0:
            lo = lo + g_four[0].astype(jnp.float32)
        else:
            hi = hi + g_four[1].astype(jnp.float32)
        g_sum[side, :16] = lo.astype(jnp.bfloat16)
        g_sum[side, 16:] = hi.astype(jnp.bfloat16)
        two.append(give(g_sum.at[side], g_two.at[side], 6 + side, k))
    wait_all(one + two)
    for side in range(2):
        grad_unit = grad_unit + g_one[side].astype(jnp.float32) + g_two[side].astype(jnp.float32)
    grad_unit = logit_scale * grad_unit
    unit_img = unit[...]
    along = jnp.sum(unit_img * grad_unit, axis=1, keepdims=True)
    gproj[c, y] = (inv_norm * (grad_unit - unit_img * along)).astype(jnp.bfloat16)

    def gp_at(slot, half):
        return gproj.at[c, slot] if half is None else gproj.at[c, slot, pl.ds(half * 16, 16)]

    gp_one = share(gp_at, y, NY, on_y, gp_s, gp_r)
    wait_all(col_copies + nt_copies)
    gp_on = pass_on(gp_at, y, NY, on_y, gp_s, gp_r, gp_one)
    finish(gp_one, gp_on)
    remote(gproj.at[c], gproj.at[c], gc_s.at[0], gc_r.at[0], sib).wait()

    def group_rows(g):
        return jnp.concatenate([gproj[0, g], gproj[1, g], gproj[0, g + NYL], gproj[1, g + NYL]], axis=0)

    weight_part = jnp.dot(nt[0], group_rows(0), preferred_element_type=jnp.float32)
    for g in range(1, NYL):
        weight_part += jnp.dot(nt[g], group_rows(g), preferred_element_type=jnp.float32)
    weight_part = weight_part.astype(jnp.bfloat16)
    slots = tile_slots()
    for i, j, tx, tz, k in slots:
        wsend[tx, tz, k] = weight_part[i * 16 : (i + 1) * 16, j * 128 : (j + 1) * 128]
    wx_copies = [
        remote(wsend.at[(x + k) % NX], wx.at[x], wx_s.at[k - 1], wx_r.at[k - 1], on_x(k)) for k in range(1, NX)
    ]
    wx[x] = wsend[x]
    rows = group_rows(yl)
    grad_normed = lax.dot_general(rows, w[...], NT, preferred_element_type=jnp.float32)
    col = (cols[0] + cols[1]) + (cols[2] + cols[3])
    grad_total = jnp.sum(rows.astype(jnp.float32) * col[:1], axis=1, keepdims=True)
    gfeat_ref[...] = (grad_normed - grad_total / 1536.0).astype(jnp.bfloat16)
    wait_all(wx_copies)
    over_x = wx[0].astype(jnp.float32)
    for k in range(1, NX):
        over_x += wx[k].astype(jnp.float32)
    zsend[...] = over_x.astype(jnp.bfloat16)
    wz_copies = [
        remote(zsend.at[(z + k) % NZ], wz.at[z], wz_s.at[k - 1], wz_r.at[k - 1], on_z(k)) for k in range(1, NZ)
    ]
    wz[z] = zsend[z]
    wait_all(wz_copies)
    over_z = wz[0].astype(jnp.float32)
    for k in range(1, NZ):
        over_z += wz[k].astype(jnp.float32)
    fin_y[yl] = over_z.astype(jnp.bfloat16)
    wait_all(
        [remote(fin_y.at[yl], fin_y.at[yl], fy_s.at[k - 1], fy_r.at[k - 1], on_yl(k)) for k in range(1, NYL)]
    )
    fin_a[z, x] = fin_y[:, 0]
    fin_b[x, z] = fin_y[:, 1]
    fa_x = [
        remote(fin_a.at[z, x], fin_a.at[z, x], fax_s.at[k - 1], fax_r.at[k - 1], on_x(k)) for k in range(1, NX)
    ]

    def fa_at(slot, half):
        return fin_a.at[slot] if half is None else fin_a.at[slot, pl.ds(half * (NX // 2), NX // 2)]

    def fb_at(slot, half):
        return fin_b.at[x, slot] if half is None else fin_b.at[x, slot, pl.ds(half * (NYL // 2), NYL // 2)]

    fb_z = share(fb_at, z, NZ, on_z, fbz_s, fbz_r)
    wait_all(fa_x)
    fa_z = share(fa_at, z, NZ, on_z, faz_s, faz_r)
    fb_on = pass_on(fb_at, z, NZ, on_z, fbz_s, fbz_r, fb_z)
    finish(fb_z, fb_on)
    fb_x = [remote(fin_b.at[x], fin_b.at[x], fbx_s.at[k - 1], fbx_r.at[k - 1], on_x(k)) for k in range(1, NX)]
    fa_on = pass_on(fa_at, z, NZ, on_z, faz_s, faz_r, fa_z)
    finish(fa_z, fa_on)
    wait_all(fb_x)
    for g in range(NYL):
        for i, j, tx, tz, k in slots:
            tile = fin_a[tz, tx, g] if k == 0 else fin_b[tx, tz, g]
            gweight_ref[g * 96 + i * 16 : g * 96 + (i + 1) * 16, j * 128 : (j + 1) * 128] = tile


def shards(features, proj_weight, texts):
    rows, width = features.shape
    e = proj_weight.shape[1]
    bf16, f32 = jnp.bfloat16, jnp.float32
    dma = pltpu.SemaphoreType.DMA
    counts = [NX - 1, 8, NX - 1, 8, 2, 3, 3, NYL - 1, 2, 8, 8, 8, 1, NX - 1, NZ - 1, NYL - 1, NX - 1, 8, NX - 1, 8]
    semaphores = [dma((3,))] + [dma((n,)) for n in counts for _ in range(2)]
    hbm = pl.BlockSpec(memory_space=pltpu.HBM)
    grad_features, grad_weight = pl.pallas_call(
        kernel,
        out_shape=(
            jax.ShapeDtypeStruct((rows, width), bf16),
            jax.ShapeDtypeStruct((width, e), bf16),
        ),
        in_specs=[hbm] * 3,
        out_specs=[pl.BlockSpec(memory_space=pltpu.VMEM)] * 2,
        scratch_shapes=[
            pltpu.VMEM((rows, width), bf16),
            pltpu.VMEM((width, e), bf16),
            pltpu.VMEM((32, e), bf16),
            pltpu.VMEM((2, 2, NX * NZ, 16, e), bf16),
            pltpu.VMEM((4, 8, 128), f32),
            pltpu.VMEM((4, 8, e), f32),
            pltpu.VMEM((rows, width), bf16),
            pltpu.VMEM((NYL, width // NYL, rows), bf16),
            pltpu.VMEM((NYL, width // NYL, rows), bf16),
            pltpu.VMEM((2, 2, 32, e), f32),
            pltpu.VMEM((2, 32, e), f32),
            pltpu.VMEM((32, e), f32),
            pltpu.VMEM((32, e), f32),
            pltpu.VMEM((NY, 32, e), bf16),
            pltpu.VMEM((NY, 32, e), f32),
            pltpu.VMEM((NY, 32, e), bf16),
            pltpu.VMEM((2, 32, e), bf16),
            pltpu.VMEM((2, 16, e), bf16),
            pltpu.VMEM((2, 32, e), bf16),
            pltpu.VMEM((2, 32, e), bf16),
            pltpu.VMEM((2, 32, e), bf16),
            pltpu.VMEM((2, NY, 32, e), bf16),
            pltpu.VMEM((NX, NZ, 2, 16, 128), bf16),
            pltpu.VMEM((NX, NZ, 2, 16, 128), bf16),
            pltpu.VMEM((NZ, 2, 16, 128), bf16),
            pltpu.VMEM((NZ, 2, 16, 128), bf16),
            pltpu.VMEM((NYL, 2, 16, 128), bf16),
            pltpu.VMEM((NZ, NX, NYL, 16, 128), bf16),
            pltpu.VMEM((NX, NZ, NYL, 16, 128), bf16),
        ]
        + semaphores,
        compiler_params=pltpu.CompilerParams(
            collective_id=0, has_side_effects=True, vmem_limit_bytes=60 << 20
        ),
        cost_estimate=pl.CostEstimate(flops=2_750_000_000, bytes_accessed=8_000_000, transcendentals=524288),
        name="head_loss",
    )(features, proj_weight, texts)
    return grad_features, grad_weight.astype(f32)


def solution(mesh):
    return jax.shard_map(
        shards,
        mesh=mesh,
        in_specs=(P("dp", "mp"), P("mp", None), P(("dp", "mp"), None)),
        out_specs=(P("dp", "mp"), P("mp", None)),
        check_vma=False,
    )
```

```python
import jax
import jax.numpy as jnp
from jax import lax
from jax.experimental import pallas as pl
from jax.experimental.pallas import tpu as pltpu
from jax.sharding import PartitionSpec as P

logit_scale = 100.0
logit_bias = -10.0
epsilon = 1e-06
NX, NYL, NZ = 4, 4, 8
NY = 2 * NYL
MESH = pl.DeviceIdType.MESH
NT = (((1,), (1,)), ((), ()))


def place(x, y, z, c):
    return ((y % NYL) * NX + x) * NZ + z, (y // NYL) * 2 + c


def unit_scale(values):
    return lax.rsqrt(jnp.sum(values * values, axis=1, keepdims=True) + epsilon)


def tile_slots():
    slots = []
    for i in range(6):
        for j in range(9):
            q = i * 9 + j
            slots.append((i, j, q % NX, (q // NX) % NZ, q // (NX * NZ)))
    return slots


def remote(src, dst, s, r, to):
    copy = pltpu.make_async_remote_copy(
        src_ref=src, dst_ref=dst, send_sem=s, recv_sem=r, device_id=to, device_id_type=MESH
    )
    copy.start()
    return copy


def wait_all(copies):
    for copy in copies:
        copy.wait()


HERE = 2


def share(at, ring, to, s, r):
    def go(index, k):
        return remote(at(HERE, None), at((HERE - k) % ring, None), s.at[index], r.at[index], to(k % ring))

    return [go(0, 2), go(1, -2), go(2, 1), go(3, -1)]


def pass_on(at, ring, to, s, r, copies):
    copies[0].wait_recv()
    on = [
        remote(at(0, None), at(7, None), s.at[4], r.at[4], to(1)),
        remote(at(0, 0), at(6, 0), s.at[5], r.at[5], to(2)),
    ]
    copies[1].wait_recv()
    on += [
        remote(at(4, None), at(5, None), s.at[6], r.at[6], to(ring - 1)),
        remote(at(4, 1), at(6, 1), s.at[7], r.at[7], to(ring - 2)),
    ]
    return on


def near(copies):
    copies[2].wait()
    copies[3].wait()


def finish(copies, on):
    copies[0].wait_send()
    copies[1].wait_send()
    wait_all(on)


def kernel(
    feat_hbm, w_hbm, text_hbm, gfeat_ref, gweight_ref,
    feat, w, text_in, txa, txb, sums, cols, normed, nt_send, nt, part, part_core, part_far, unit, img,
    grad, gs, g_three, g_four, g_one, g_sum, g_two, gproj, wsend, wx, zsend, wz, fin_y, fin_a, fin_b,
    in_s, ax_s, ax_r, az_s, az_r, bx_s, bx_r, bz_s, bz_r, ts_s, ts_r,
    su_s, su_r, co_s, co_r, nt_s, nt_r, pc_s, pc_r, im_s, im_r,
    gy_s, gy_r, gp_s, gp_r, gc_s, gc_r, wx_s, wx_r, wz_s, wz_r, fy_s, fy_r,
    fax_s, fax_r, faz_s, faz_r, fbx_s, fbx_r, fbz_s, fbz_r,
):
    dp = lax.axis_index("dp")
    mp = lax.axis_index("mp")
    yl = dp // (NX * NZ)
    x = (dp // NZ) % NX
    z = dp % NZ
    yh = mp // 2
    c = mp % 2
    y = yh * NYL + yl
    sib = place(x, y, z, 1 - c)
    y_far = (y + NYL) % NY
    far = place(x, y_far, z, c)
    far_sib = place(x, y_far, z, 1 - c)

    def on_y(k):
        return place(x, (y + k) % NY, z, c)

    def on_yl(k):
        return place(x, yh * NYL + (yl + k) % NYL, z, c)

    def on_x(k):
        return place((x + k) % NX, y, z, c)

    def on_z(k):
        return place(x, y, (z + k) % NZ, c)

    barrier = pltpu.get_barrier_semaphore()
    others = [sib, far_sib]
    others += [on_y(k) for k in range(1, NY)]
    others += [on_x(k) for k in range(1, NX)]
    others += [on_z(k) for k in range(1, NZ)]
    for other in others:
        pl.semaphore_signal(barrier, inc=1, device_id=other, device_id_type=MESH)

    text_load = pltpu.make_async_copy(text_hbm, text_in, in_s.at[0])
    feat_load = pltpu.make_async_copy(feat_hbm, feat, in_s.at[1])
    w_load = pltpu.make_async_copy(w_hbm, w, in_s.at[2])
    feat_load.start()
    text_load.start()
    w_load.start()

    feat_load.wait()
    inputs = feat[...].astype(jnp.float32)
    row_sum = jnp.sum(inputs, axis=1, keepdims=True)
    sums[mp] = jnp.broadcast_to(row_sum, (128, 128)).T[:8]
    text_load.wait()
    text = text_in[...].astype(jnp.float32)
    own_text = (text * unit_scale(text)).astype(jnp.bfloat16)
    txa[c, HERE, x] = own_text[:16]
    txb[c, x, HERE] = own_text[16:]
    pl.semaphore_wait(barrier, len(others))

    mates = [sib, far, far_sib]
    sum_copies = [remote(sums.at[mp], sums.at[mp], su_s.at[k], su_r.at[k], to) for k, to in enumerate(mates)]

    own_a = txa.at[c, HERE, x]
    a_x = [remote(own_a, own_a, ax_s.at[k - 1], ax_r.at[k - 1], on_x(k)) for k in range(1, NX)]

    def a_at(r, half):
        return txa.at[c, r] if half is None else txa.at[c, r, pl.ds(half * (NX // 2), NX // 2)]

    def b_at(r, half):
        if half is None:
            return txb.at[c, x, r]
        return txb.at[c, x, r, :, pl.ds(0, 640)] if half == 0 else txb.at[c, x, r, :, pl.ds(640, 512)]

    def b_to_x(lo, count, index):
        block = txb.at[c, x, pl.ds(lo, count)]
        return [
            remote(block, block, bx_s.at[index + k - 1], bx_r.at[index + k - 1], on_x(k)) for k in range(1, NX)
        ]

    def to_sib(block, index):
        return remote(block, block, ts_s.at[index], ts_r.at[index], sib)

    b_z = share(b_at, NZ, on_z, bz_s, bz_r)

    w_load.wait()
    weights = w[...]
    cols[mp] = jnp.broadcast_to(
        jnp.sum(weights.astype(jnp.float32), axis=0, keepdims=True), (8, weights.shape[1])
    )

    wait_all(a_x)
    a_z = share(a_at, NZ, on_z, az_s, az_r)
    wait_all(sum_copies)
    total = (sums[0] + sums[1]) + (sums[2] + sums[3])
    mean_in = jnp.broadcast_to(total[:1] / 1536.0, (128, 128)).T[:, :1]
    centred = inputs - mean_in
    normed[...] = centred.astype(jnp.bfloat16)
    partial = jnp.dot(normed[...], weights, preferred_element_type=jnp.float32)
    for h in range(2):
        for b in range(2):
            part[b, h] = partial[(h * 2 + b) * 32 : (h * 2 + b + 1) * 32]
    core_copy = remote(part.at[1 - c], part_core, pc_s.at[0], pc_r.at[0], sib)
    b_on = pass_on(b_at, NZ, on_z, bz_s, bz_r, b_z)
    core_copy.wait()
    part[c, 1 - yh] += part_core[1 - yh]
    far_copy = remote(part.at[c, 1 - yh], part_far, pc_s.at[1], pc_r.at[1], far)
    near(b_z)
    b_x = b_to_x(0, 5, 0)
    turned = centred.T.astype(jnp.bfloat16)
    for g in range(NYL):
        nt_send[g] = turned[g * 96 : (g + 1) * 96]
    nt[yl] = nt_send[yl]
    a_on = pass_on(a_at, NZ, on_z, az_s, az_r, a_z)
    finish(b_z, b_on)
    b_x2 = b_to_x(5, 3, 3)
    far_copy.wait()
    project = part[c, yh] + part_core[yh] + part_far[...]
    inv_norm = unit_scale(project)
    unit_img = project * inv_norm
    unit[...] = unit_img
    img[HERE] = unit_img.astype(jnp.bfloat16)

    def img_at(r, half):
        return img.at[r] if half is None else img.at[r, pl.ds(half * 16, 16)]

    img_one = share(img_at, NY, on_y, im_s, im_r)
    near(a_z)
    to_core = [to_sib(txa.at[c, pl.ds(0, 5)], 0)]
    img_on = pass_on(img_at, NY, on_y, im_s, im_r, img_one)
    wait_all(b_x)
    to_core += [to_sib(txb.at[c, :, pl.ds(0, 5)], 1)]
    finish(a_z, a_on)
    to_core += [to_sib(txa.at[c, pl.ds(5, 3)], 2)]
    wait_all(b_x2)
    to_core += [to_sib(txb.at[c, :, pl.ds(5, 3)], 3)]
    near(img_one)
    finish(img_one, img_on)
    col_copies = [remote(cols.at[mp], cols.at[mp], co_s.at[k], co_r.at[k], to) for k, to in enumerate(mates)]
    nt_copies = [
        remote(nt_send.at[(yl + k) % NYL], nt.at[yl], nt_s.at[k - 1], nt_r.at[k - 1], on_yl(k))
        for k in range(1, NYL)
    ]

    def add_texts(block, first):
        texts = block[...].reshape(NX * NZ * 16, -1)
        images = img[...].reshape(NY * 32, -1)
        score = lax.dot_general(images, texts, NT, preferred_element_type=jnp.float32)
        slope = jax.nn.sigmoid(logit_scale * score + logit_bias).astype(jnp.bfloat16)
        terms = jnp.dot(slope, texts, preferred_element_type=jnp.float32).reshape(grad.shape)
        grad[...] = terms if first else grad[...] + terms

    add_texts(txa.at[c], True)
    add_texts(txb.at[c], False)
    wait_all(to_core)
    add_texts(txa.at[1 - c], False)
    add_texts(txb.at[1 - c], False)

    for r in (5, 7, 6, 3, 1):
        gs[r] = grad[r].astype(jnp.bfloat16)

    def give(src, dst, index, k):
        return remote(src, dst, gy_s.at[index], gy_r.at[index], on_y(k))

    three = [give(gs.at[5], g_three.at[0], 0, 1), give(gs.at[7], g_three.at[1], 1, NY - 1)]
    four = [
        give(gs.at[6, pl.ds(0, 16)], g_four.at[0], 2, 2),
        give(gs.at[6, pl.ds(16, 16)], g_four.at[1], 3, NY - 2),
    ]
    one = [give(gs.at[3], g_one.at[0], 4, 1), give(gs.at[1], g_one.at[1], 5, NY - 1)]
    own_b16 = img[HERE].astype(jnp.float32)
    own_t = jnp.concatenate([txa[c, HERE, x], txb[c, x, HERE]], axis=0).astype(jnp.float32)
    own_logit = logit_scale * jnp.sum(own_b16 * own_t, axis=1, keepdims=True) + logit_bias
    wrong = jax.nn.sigmoid(own_logit).astype(jnp.bfloat16).astype(jnp.float32)
    right = (-jax.nn.sigmoid(-own_logit)).astype(jnp.bfloat16).astype(jnp.float32)
    grad_unit = grad[HERE] + (right - wrong) * own_t
    wsend[...] = jnp.zeros_like(wsend)
    two = []
    for side, k in ((0, 2), (1, NY - 2)):
        three[side].wait()
        four[side].wait()
        far_sum = grad[(HERE + k) % NY] + g_three[side].astype(jnp.float32)
        lo, hi = far_sum[:16], far_sum[16:]
        if side == 0:
            lo = lo + g_four[0].astype(jnp.float32)
        else:
            hi = hi + g_four[1].astype(jnp.float32)
        g_sum[side, :16] = lo.astype(jnp.bfloat16)
        g_sum[side, 16:] = hi.astype(jnp.bfloat16)
        two.append(give(g_sum.at[side], g_two.at[side], 6 + side, k))
    wait_all(one + two)
    for side in range(2):
        grad_unit = grad_unit + g_one[side].astype(jnp.float32) + g_two[side].astype(jnp.float32)
    grad_unit = logit_scale * grad_unit
    unit_img = unit[...]
    along = jnp.sum(unit_img * grad_unit, axis=1, keepdims=True)
    gproj[c, HERE] = (inv_norm * (grad_unit - unit_img * along)).astype(jnp.bfloat16)

    def gp_at(r, half):
        return gproj.at[c, r] if half is None else gproj.at[c, r, pl.ds(half * 16, 16)]

    def gp_to_sib(lo, count, index):
        block = gproj.at[c, pl.ds(lo, count)]
        return remote(block, block, gc_s.at[index], gc_r.at[index], sib)

    gp_one = share(gp_at, NY, on_y, gp_s, gp_r)
    wait_all(col_copies + nt_copies)
    gp_on = pass_on(gp_at, NY, on_y, gp_s, gp_r, gp_one)
    near(gp_one)
    gp_core = [gp_to_sib(0, 5, 0)]
    finish(gp_one, gp_on)
    gp_core += [gp_to_sib(5, 3, 1)]
    wait_all(gp_core)

    def group_rows(g):
        low, high = (g - y + HERE + NY) % NY, (g - y + HERE + NY + NYL) % NY
        return jnp.concatenate([gproj[0, low], gproj[1, low], gproj[0, high], gproj[1, high]], axis=0)

    weight_part = jnp.dot(nt[0], group_rows(0), preferred_element_type=jnp.float32)
    for g in range(1, NYL):
        weight_part += jnp.dot(nt[g], group_rows(g), preferred_element_type=jnp.float32)
    weight_part = weight_part.astype(jnp.bfloat16)
    slots = tile_slots()
    for i, j, tx, tz, k in slots:
        wsend[tx, tz, k] = weight_part[i * 16 : (i + 1) * 16, j * 128 : (j + 1) * 128]
    wx_copies = [
        remote(wsend.at[(x + k) % NX], wx.at[x], wx_s.at[k - 1], wx_r.at[k - 1], on_x(k)) for k in range(1, NX)
    ]
    wx[x] = wsend[x]
    rows = group_rows(yl)
    grad_normed = lax.dot_general(rows, w[...], NT, preferred_element_type=jnp.float32)
    col = (cols[0] + cols[1]) + (cols[2] + cols[3])
    grad_total = jnp.sum(rows.astype(jnp.float32) * col[:1], axis=1, keepdims=True)
    gfeat_ref[...] = (grad_normed - grad_total / 1536.0).astype(jnp.bfloat16)
    wait_all(wx_copies)
    over_x = wx[0].astype(jnp.float32)
    for k in range(1, NX):
        over_x += wx[k].astype(jnp.float32)
    zsend[...] = over_x.astype(jnp.bfloat16)
    wz_copies = [
        remote(zsend.at[(z + k) % NZ], wz.at[z], wz_s.at[k - 1], wz_r.at[k - 1], on_z(k)) for k in range(1, NZ)
    ]
    wz[z] = zsend[z]
    wait_all(wz_copies)
    over_z = wz[0].astype(jnp.float32)
    for k in range(1, NZ):
        over_z += wz[k].astype(jnp.float32)
    fin_y[yl] = over_z.astype(jnp.bfloat16)
    wait_all(
        [remote(fin_y.at[yl], fin_y.at[yl], fy_s.at[k - 1], fy_r.at[k - 1], on_yl(k)) for k in range(1, NYL)]
    )
    fin_a[HERE, x] = fin_y[:, 0]
    fin_b[x, HERE] = fin_y[:, 1]
    own_fa = fin_a.at[HERE, x]
    fa_x = [remote(own_fa, own_fa, fax_s.at[k - 1], fax_r.at[k - 1], on_x(k)) for k in range(1, NX)]

    def fa_at(r, half):
        return fin_a.at[r] if half is None else fin_a.at[r, pl.ds(half * (NX // 2), NX // 2)]

    def fb_at(r, half):
        return fin_b.at[x, r] if half is None else fin_b.at[x, r, pl.ds(half * (NYL // 2), NYL // 2)]

    def fb_to_x(lo, count, index):
        block = fin_b.at[x, pl.ds(lo, count)]
        return [
            remote(block, block, fbx_s.at[index + k - 1], fbx_r.at[index + k - 1], on_x(k)) for k in range(1, NX)
        ]

    fb_z = share(fb_at, NZ, on_z, fbz_s, fbz_r)
    wait_all(fa_x)
    fa_z = share(fa_at, NZ, on_z, faz_s, faz_r)
    fb_on = pass_on(fb_at, NZ, on_z, fbz_s, fbz_r, fb_z)
    near(fb_z)
    fb_x = fb_to_x(0, 5, 0)
    fa_on = pass_on(fa_at, NZ, on_z, faz_s, faz_r, fa_z)
    finish(fb_z, fb_on)
    fb_x += fb_to_x(5, 3, 3)
    near(fa_z)
    finish(fa_z, fa_on)
    wait_all(fb_x)
    at_z = [(tz - z + HERE + NZ) % NZ for tz in range(NZ)]
    for g in range(NYL):
        for i, j, tx, tz, k in slots:
            tile = fin_a[at_z[tz], tx, g] if k == 0 else fin_b[tx, at_z[tz], g]
            gweight_ref[g * 96 + i * 16 : g * 96 + (i + 1) * 16, j * 128 : (j + 1) * 128] = tile


def shards(features, proj_weight, texts):
    rows, width = features.shape
    e = proj_weight.shape[1]
    bf16, f32 = jnp.bfloat16, jnp.float32
    dma = pltpu.SemaphoreType.DMA
    counts = [3, 8, 6, 8, 4, 3, 3, NYL - 1, 2, 8, 8, 8, 2, NX - 1, NZ - 1, NYL - 1, 3, 8, 6, 8]
    semaphores = [dma((3,))] + [dma((n,)) for n in counts for _ in range(2)]
    hbm = pl.BlockSpec(memory_space=pltpu.HBM)
    grad_features, grad_weight = pl.pallas_call(
        kernel,
        out_shape=(
            jax.ShapeDtypeStruct((rows, width), bf16),
            jax.ShapeDtypeStruct((width, e), bf16),
        ),
        in_specs=[hbm] * 3,
        out_specs=[pl.BlockSpec(memory_space=pltpu.VMEM)] * 2,
        scratch_shapes=[
            pltpu.VMEM((rows, width), bf16),
            pltpu.VMEM((width, e), bf16),
            pltpu.VMEM((32, e), bf16),
            pltpu.VMEM((2, NZ, NX, 16, e), bf16),
            pltpu.VMEM((2, NX, NZ, 16, e), bf16),
            pltpu.VMEM((4, 8, 128), f32),
            pltpu.VMEM((4, 8, e), f32),
            pltpu.VMEM((rows, width), bf16),
            pltpu.VMEM((NYL, width // NYL, rows), bf16),
            pltpu.VMEM((NYL, width // NYL, rows), bf16),
            pltpu.VMEM((2, 2, 32, e), f32),
            pltpu.VMEM((2, 32, e), f32),
            pltpu.VMEM((32, e), f32),
            pltpu.VMEM((32, e), f32),
            pltpu.VMEM((NY, 32, e), bf16),
            pltpu.VMEM((NY, 32, e), f32),
            pltpu.VMEM((NY, 32, e), bf16),
            pltpu.VMEM((2, 32, e), bf16),
            pltpu.VMEM((2, 16, e), bf16),
            pltpu.VMEM((2, 32, e), bf16),
            pltpu.VMEM((2, 32, e), bf16),
            pltpu.VMEM((2, 32, e), bf16),
            pltpu.VMEM((2, NY, 32, e), bf16),
            pltpu.VMEM((NX, NZ, 2, 16, 128), bf16),
            pltpu.VMEM((NX, NZ, 2, 16, 128), bf16),
            pltpu.VMEM((NZ, 2, 16, 128), bf16),
            pltpu.VMEM((NZ, 2, 16, 128), bf16),
            pltpu.VMEM((NYL, 2, 16, 128), bf16),
            pltpu.VMEM((NZ, NX, NYL, 16, 128), bf16),
            pltpu.VMEM((NX, NZ, NYL, 16, 128), bf16),
        ]
        + semaphores,
        compiler_params=pltpu.CompilerParams(
            collective_id=0, has_side_effects=True, vmem_limit_bytes=60 << 20
        ),
        cost_estimate=pl.CostEstimate(flops=2_750_000_000, bytes_accessed=8_000_000, transcendentals=524288),
        name="head_loss",
    )(features, proj_weight, texts)
    return grad_features, grad_weight.astype(f32)


def solution(mesh):
    return jax.shard_map(
        shards,
        mesh=mesh,
        in_specs=(P("dp", "mp"), P("mp", None), P(("dp", "mp"), None)),
        out_specs=(P("dp", "mp"), P("mp", None)),
        check_vma=False,
    )
```

```python
import jax
import jax.numpy as jnp
from jax import lax
from jax.experimental import pallas as pl
from jax.experimental.pallas import tpu as pltpu
from jax.sharding import PartitionSpec as P

logit_scale = 100.0
logit_bias = -10.0
epsilon = 1e-06
NX, NYL, NZ = 4, 4, 8
NY = 2 * NYL
MESH = pl.DeviceIdType.MESH
NT = (((1,), (1,)), ((), ()))


def place(x, y, z, c):
    return ((y % NYL) * NX + x) * NZ + z, (y // NYL) * 2 + c


def unit_scale(values):
    return lax.rsqrt(jnp.sum(values * values, axis=1, keepdims=True) + epsilon)


def tile_slots():
    slots = []
    for i in range(6):
        for j in range(9):
            q = i * 9 + j
            slots.append((i, j, q % NX, (q // NX) % NZ, q // (NX * NZ)))
    return slots


def remote(src, dst, s, r, to):
    copy = pltpu.make_async_remote_copy(
        src_ref=src, dst_ref=dst, send_sem=s, recv_sem=r, device_id=to, device_id_type=MESH
    )
    copy.start()
    return copy


def wait_all(copies):
    for copy in copies:
        copy.wait()


HERE = 2


def share(at, ring, to, s, r):
    def go(index, k):
        return remote(at(HERE, None), at((HERE - k) % ring, None), s.at[index], r.at[index], to(k % ring))

    return [go(0, 2), go(1, -2), go(2, 1), go(3, -1)]


def pass_on(at, ring, to, s, r, copies):
    copies[0].wait_recv()
    on = [
        remote(at(0, None), at(7, None), s.at[4], r.at[4], to(1)),
        remote(at(0, 0), at(6, 0), s.at[5], r.at[5], to(2)),
    ]
    copies[1].wait_recv()
    on += [
        remote(at(4, None), at(5, None), s.at[6], r.at[6], to(ring - 1)),
        remote(at(4, 1), at(6, 1), s.at[7], r.at[7], to(ring - 2)),
    ]
    return on


def near(copies):
    copies[2].wait()
    copies[3].wait()


def finish(copies, on):
    copies[0].wait_send()
    copies[1].wait_send()
    wait_all(on)


def kernel(
    feat_hbm, w_hbm, text_hbm, gfeat_ref, gweight_ref,
    feat, w, text_in, txa, txb, sums, cols, nt_send, nt, part, part_core, part_far, unit, img,
    grad, gs, g_three, g_four, g_one, g_sum, g_two, gproj, wsend, wx, zsend, wz, fin_y, fin_a, fin_b,
    in_s, ax_s, ax_r, az_s, az_r, bx_s, bx_r, bz_s, bz_r, ts_s, ts_r,
    su_s, su_r, co_s, co_r, nt_s, nt_r, pc_s, pc_r, im_s, im_r,
    gy_s, gy_r, gp_s, gp_r, gc_s, gc_r, wx_s, wx_r, wz_s, wz_r, fy_s, fy_r,
    fax_s, fax_r, faz_s, faz_r, fbx_s, fbx_r, fbz_s, fbz_r,
):
    dp = lax.axis_index("dp")
    mp = lax.axis_index("mp")
    yl = dp // (NX * NZ)
    x = (dp // NZ) % NX
    z = dp % NZ
    yh = mp // 2
    c = mp % 2
    y = yh * NYL + yl
    sib = place(x, y, z, 1 - c)
    y_far = (y + NYL) % NY
    far = place(x, y_far, z, c)
    far_sib = place(x, y_far, z, 1 - c)

    def on_y(k):
        return place(x, (y + k) % NY, z, c)

    def on_yl(k):
        return place(x, yh * NYL + (yl + k) % NYL, z, c)

    def on_x(k):
        return place((x + k) % NX, y, z, c)

    def on_z(k):
        return place(x, y, (z + k) % NZ, c)

    barrier = pltpu.get_barrier_semaphore()
    others = [sib, far_sib]
    others += [on_y(k) for k in range(1, NY)]
    others += [on_x(k) for k in range(1, NX)]
    others += [on_z(k) for k in range(1, NZ)]
    for other in others:
        pl.semaphore_signal(barrier, inc=1, device_id=other, device_id_type=MESH)

    text_load = pltpu.make_async_copy(text_hbm, text_in, in_s.at[0])
    feat_load = pltpu.make_async_copy(feat_hbm, feat, in_s.at[1])
    w_load = pltpu.make_async_copy(w_hbm, w, in_s.at[2])
    feat_load.start()
    w_load.start()
    text_load.start()

    e = w.shape[1]
    feat_load.wait()
    inputs = feat[...].astype(jnp.float32)
    row_sum = jnp.broadcast_to(jnp.sum(inputs, axis=1, keepdims=True), (128, 128))
    sums[mp] = row_sum.T[:8]
    w_load.wait()
    partial = jnp.dot(feat[...], w[...], preferred_element_type=jnp.float32)
    for h in range(2):
        for b in range(2):
            lo = (h * 2 + b) * 32
            part[b, h, :, :e] = partial[lo : lo + 32]
            part[b, h, :, e:] = row_sum[lo : lo + 32]
    cols[mp] = jnp.sum(w[...].astype(jnp.float32), axis=0, keepdims=True)
    text_load.wait()
    text = text_in[...].astype(jnp.float32)
    own_text = (text * unit_scale(text)).astype(jnp.bfloat16)
    txa[c, HERE, x] = own_text[:16]
    txb[c, x, HERE] = own_text[16:]
    pl.semaphore_wait(barrier, len(others))

    core_copy = remote(part.at[1 - c], part_core, pc_s.at[0], pc_r.at[0], sib)
    mates = [sib, far, far_sib]
    col_copies = [remote(cols.at[mp], cols.at[mp], co_s.at[k], co_r.at[k], to) for k, to in enumerate(mates)]

    own_a = txa.at[c, HERE, x]
    a_x = [remote(own_a, own_a, ax_s.at[k - 1], ax_r.at[k - 1], on_x(k)) for k in range(1, NX)]

    def a_at(r, half):
        return txa.at[c, r] if half is None else txa.at[c, r, pl.ds(half * (NX // 2), NX // 2)]

    def b_at(r, half):
        if half is None:
            return txb.at[c, x, r]
        return txb.at[c, x, r, :, pl.ds(0, 640)] if half == 0 else txb.at[c, x, r, :, pl.ds(640, 512)]

    def b_to_x(lo, count, index):
        block = txb.at[c, x, pl.ds(lo, count)]
        return [
            remote(block, block, bx_s.at[index + k - 1], bx_r.at[index + k - 1], on_x(k)) for k in range(1, NX)
        ]

    def to_sib(block, index):
        return remote(block, block, ts_s.at[index], ts_r.at[index], sib)

    b_z = share(b_at, NZ, on_z, bz_s, bz_r)

    sum_copies = [remote(sums.at[mp], sums.at[mp], su_s.at[k], su_r.at[k], to) for k, to in enumerate(mates)]

    core_copy.wait()
    part[c, 1 - yh] += part_core[1 - yh]
    far_copy = remote(part.at[c, 1 - yh], part_far, pc_s.at[1], pc_r.at[1], far)
    wait_all(a_x)
    a_z = share(a_at, NZ, on_z, az_s, az_r)
    b_on = pass_on(b_at, NZ, on_z, bz_s, bz_r, b_z)
    near(b_z)
    b_x = b_to_x(0, 5, 0)
    wait_all(col_copies)
    col = (cols[0] + cols[1]) + (cols[2] + cols[3])
    far_copy.wait()
    joined = part[c, yh] + part_core[yh] + part_far[...]
    project = joined[:, :e] - (joined[:, e : e + 1] / 1536.0) * col
    inv_norm = unit_scale(project)
    unit_img = project * inv_norm
    unit[...] = unit_img
    img[HERE] = unit_img.astype(jnp.bfloat16)

    def img_at(r, half):
        return img.at[r] if half is None else img.at[r, pl.ds(half * 16, 16)]

    img_one = share(img_at, NY, on_y, im_s, im_r)
    finish(b_z, b_on)
    b_x2 = b_to_x(5, 3, 3)
    a_on = pass_on(a_at, NZ, on_z, az_s, az_r, a_z)
    img_on = pass_on(img_at, NY, on_y, im_s, im_r, img_one)
    wait_all(sum_copies)
    total = (sums[0] + sums[1]) + (sums[2] + sums[3])
    mean_in = jnp.broadcast_to(total[:1] / 1536.0, (128, 128)).T[:, :1]
    turned = (feat[...].astype(jnp.float32) - mean_in).T.astype(jnp.bfloat16)
    for g in range(NYL):
        nt_send[g] = turned[g * 96 : (g + 1) * 96]
    nt[yl] = nt_send[yl]
    near(a_z)
    to_core = [to_sib(txa.at[c, pl.ds(0, 5)], 0)]
    wait_all(b_x)
    to_core += [to_sib(txb.at[c, :, pl.ds(0, 5)], 1)]
    near(img_one)
    finish(img_one, img_on)
    finish(a_z, a_on)
    to_core += [to_sib(txa.at[c, pl.ds(5, 3)], 2)]
    wait_all(b_x2)
    to_core += [to_sib(txb.at[c, :, pl.ds(5, 3)], 3)]
    nt_copies = [
        remote(nt_send.at[(yl + k) % NYL], nt.at[yl], nt_s.at[k - 1], nt_r.at[k - 1], on_yl(k))
        for k in range(1, NYL)
    ]

    def add_texts(block, first):
        texts = block[...].reshape(NX * NZ * 16, -1)
        images = img[...].reshape(NY * 32, -1)
        score = lax.dot_general(images, texts, NT, preferred_element_type=jnp.float32)
        slope = jax.nn.sigmoid(logit_scale * score + logit_bias).astype(jnp.bfloat16)
        terms = jnp.dot(slope, texts, preferred_element_type=jnp.float32).reshape(grad.shape)
        grad[...] = terms if first else grad[...] + terms

    add_texts(txa.at[c], True)
    add_texts(txb.at[c], False)
    wait_all(to_core)
    add_texts(txa.at[1 - c], False)
    add_texts(txb.at[1 - c], False)

    for r in (5, 7, 6, 3, 1):
        gs[r] = grad[r].astype(jnp.bfloat16)

    def give(src, dst, index, k):
        return remote(src, dst, gy_s.at[index], gy_r.at[index], on_y(k))

    three = [give(gs.at[5], g_three.at[0], 0, 1), give(gs.at[7], g_three.at[1], 1, NY - 1)]
    four = [
        give(gs.at[6, pl.ds(0, 16)], g_four.at[0], 2, 2),
        give(gs.at[6, pl.ds(16, 16)], g_four.at[1], 3, NY - 2),
    ]
    one = [give(gs.at[3], g_one.at[0], 4, 1), give(gs.at[1], g_one.at[1], 5, NY - 1)]
    own_b16 = img[HERE].astype(jnp.float32)
    own_t = jnp.concatenate([txa[c, HERE, x], txb[c, x, HERE]], axis=0).astype(jnp.float32)
    own_logit = logit_scale * jnp.sum(own_b16 * own_t, axis=1, keepdims=True) + logit_bias
    wrong = jax.nn.sigmoid(own_logit).astype(jnp.bfloat16).astype(jnp.float32)
    right = (-jax.nn.sigmoid(-own_logit)).astype(jnp.bfloat16).astype(jnp.float32)
    grad_unit = grad[HERE] + (right - wrong) * own_t
    wsend[...] = jnp.zeros_like(wsend)
    two = []
    for side, k in ((0, 2), (1, NY - 2)):
        three[side].wait()
        four[side].wait()
        far_sum = grad[(HERE + k) % NY] + g_three[side].astype(jnp.float32)
        lo, hi = far_sum[:16], far_sum[16:]
        if side == 0:
            lo = lo + g_four[0].astype(jnp.float32)
        else:
            hi = hi + g_four[1].astype(jnp.float32)
        g_sum[side, :16] = lo.astype(jnp.bfloat16)
        g_sum[side, 16:] = hi.astype(jnp.bfloat16)
        two.append(give(g_sum.at[side], g_two.at[side], 6 + side, k))
    wait_all(one + two)
    for side in range(2):
        grad_unit = grad_unit + g_one[side].astype(jnp.float32) + g_two[side].astype(jnp.float32)
    grad_unit = logit_scale * grad_unit
    unit_img = unit[...]
    along = jnp.sum(unit_img * grad_unit, axis=1, keepdims=True)
    gproj[c, HERE] = (inv_norm * (grad_unit - unit_img * along)).astype(jnp.bfloat16)

    def gp_at(r, half):
        return gproj.at[c, r] if half is None else gproj.at[c, r, pl.ds(half * 16, 16)]

    def gp_to_sib(lo, count, index):
        block = gproj.at[c, pl.ds(lo, count)]
        return remote(block, block, gc_s.at[index], gc_r.at[index], sib)

    gp_one = share(gp_at, NY, on_y, gp_s, gp_r)
    wait_all(nt_copies)
    gp_on = pass_on(gp_at, NY, on_y, gp_s, gp_r, gp_one)
    near(gp_one)
    gp_core = [gp_to_sib(0, 5, 0)]
    finish(gp_one, gp_on)
    gp_core += [gp_to_sib(5, 3, 1)]
    wait_all(gp_core)

    def group_rows(g):
        low, high = (g - y + HERE + NY) % NY, (g - y + HERE + NY + NYL) % NY
        return jnp.concatenate([gproj[0, low], gproj[1, low], gproj[0, high], gproj[1, high]], axis=0)

    weight_part = jnp.dot(nt[0], group_rows(0), preferred_element_type=jnp.float32)
    for g in range(1, NYL):
        weight_part += jnp.dot(nt[g], group_rows(g), preferred_element_type=jnp.float32)
    weight_part = weight_part.astype(jnp.bfloat16)
    slots = tile_slots()
    for i, j, tx, tz, k in slots:
        wsend[tx, tz, k] = weight_part[i * 16 : (i + 1) * 16, j * 128 : (j + 1) * 128]
    wx_copies = [
        remote(wsend.at[(x + k) % NX], wx.at[x], wx_s.at[k - 1], wx_r.at[k - 1], on_x(k)) for k in range(1, NX)
    ]
    wx[x] = wsend[x]
    rows = group_rows(yl)
    grad_normed = lax.dot_general(rows, w[...], NT, preferred_element_type=jnp.float32)
    grad_total = jnp.sum(rows.astype(jnp.float32) * col, axis=1, keepdims=True)
    gfeat_ref[...] = (grad_normed - grad_total / 1536.0).astype(jnp.bfloat16)
    wait_all(wx_copies)
    over_x = wx[0].astype(jnp.float32)
    for k in range(1, NX):
        over_x += wx[k].astype(jnp.float32)
    zsend[...] = over_x.astype(jnp.bfloat16)
    wz_copies = [
        remote(zsend.at[(z + k) % NZ], wz.at[z], wz_s.at[k - 1], wz_r.at[k - 1], on_z(k)) for k in range(1, NZ)
    ]
    wz[z] = zsend[z]
    wait_all(wz_copies)
    over_z = wz[0].astype(jnp.float32)
    for k in range(1, NZ):
        over_z += wz[k].astype(jnp.float32)
    fin_y[yl] = over_z.astype(jnp.bfloat16)
    wait_all(
        [remote(fin_y.at[yl], fin_y.at[yl], fy_s.at[k - 1], fy_r.at[k - 1], on_yl(k)) for k in range(1, NYL)]
    )
    fin_a[HERE, x] = fin_y[:, 0]
    fin_b[x, HERE] = fin_y[:, 1]
    own_fa = fin_a.at[HERE, x]
    fa_x = [remote(own_fa, own_fa, fax_s.at[k - 1], fax_r.at[k - 1], on_x(k)) for k in range(1, NX)]

    def fa_at(r, half):
        return fin_a.at[r] if half is None else fin_a.at[r, pl.ds(half * (NX // 2), NX // 2)]

    def fb_at(r, half):
        return fin_b.at[x, r] if half is None else fin_b.at[x, r, pl.ds(half * (NYL // 2), NYL // 2)]

    def fb_to_x(lo, count, index):
        block = fin_b.at[x, pl.ds(lo, count)]
        return [
            remote(block, block, fbx_s.at[index + k - 1], fbx_r.at[index + k - 1], on_x(k)) for k in range(1, NX)
        ]

    fb_z = share(fb_at, NZ, on_z, fbz_s, fbz_r)
    wait_all(fa_x)
    fa_z = share(fa_at, NZ, on_z, faz_s, faz_r)
    fb_on = pass_on(fb_at, NZ, on_z, fbz_s, fbz_r, fb_z)
    near(fb_z)
    fb_x = fb_to_x(0, 5, 0)
    fa_on = pass_on(fa_at, NZ, on_z, faz_s, faz_r, fa_z)
    finish(fb_z, fb_on)
    fb_x += fb_to_x(5, 3, 3)
    near(fa_z)
    finish(fa_z, fa_on)
    wait_all(fb_x)
    at_z = [(tz - z + HERE + NZ) % NZ for tz in range(NZ)]
    for g in range(NYL):
        for i, j, tx, tz, k in slots:
            tile = fin_a[at_z[tz], tx, g] if k == 0 else fin_b[tx, at_z[tz], g]
            gweight_ref[g * 96 + i * 16 : g * 96 + (i + 1) * 16, j * 128 : (j + 1) * 128] = tile


def shards(features, proj_weight, texts):
    rows, width = features.shape
    e = proj_weight.shape[1]
    bf16, f32 = jnp.bfloat16, jnp.float32
    dma = pltpu.SemaphoreType.DMA
    counts = [3, 8, 6, 8, 4, 3, 3, NYL - 1, 2, 8, 8, 8, 2, NX - 1, NZ - 1, NYL - 1, 3, 8, 6, 8]
    semaphores = [dma((3,))] + [dma((n,)) for n in counts for _ in range(2)]
    hbm = pl.BlockSpec(memory_space=pltpu.HBM)
    grad_features, grad_weight = pl.pallas_call(
        kernel,
        out_shape=(
            jax.ShapeDtypeStruct((rows, width), bf16),
            jax.ShapeDtypeStruct((width, e), bf16),
        ),
        in_specs=[hbm] * 3,
        out_specs=[pl.BlockSpec(memory_space=pltpu.VMEM)] * 2,
        scratch_shapes=[
            pltpu.VMEM((rows, width), bf16),
            pltpu.VMEM((width, e), bf16),
            pltpu.VMEM((32, e), bf16),
            pltpu.VMEM((2, NZ, NX, 16, e), bf16),
            pltpu.VMEM((2, NX, NZ, 16, e), bf16),
            pltpu.VMEM((4, 8, 128), f32),
            pltpu.VMEM((4, 1, e), f32),
            pltpu.VMEM((NYL, width // NYL, rows), bf16),
            pltpu.VMEM((NYL, width // NYL, rows), bf16),
            pltpu.VMEM((2, 2, 32, e + 128), f32),
            pltpu.VMEM((2, 32, e + 128), f32),
            pltpu.VMEM((32, e + 128), f32),
            pltpu.VMEM((32, e), f32),
            pltpu.VMEM((NY, 32, e), bf16),
            pltpu.VMEM((NY, 32, e), f32),
            pltpu.VMEM((NY, 32, e), bf16),
            pltpu.VMEM((2, 32, e), bf16),
            pltpu.VMEM((2, 16, e), bf16),
            pltpu.VMEM((2, 32, e), bf16),
            pltpu.VMEM((2, 32, e), bf16),
            pltpu.VMEM((2, 32, e), bf16),
            pltpu.VMEM((2, NY, 32, e), bf16),
            pltpu.VMEM((NX, NZ, 2, 16, 128), bf16),
            pltpu.VMEM((NX, NZ, 2, 16, 128), bf16),
            pltpu.VMEM((NZ, 2, 16, 128), bf16),
            pltpu.VMEM((NZ, 2, 16, 128), bf16),
            pltpu.VMEM((NYL, 2, 16, 128), bf16),
            pltpu.VMEM((NZ, NX, NYL, 16, 128), bf16),
            pltpu.VMEM((NX, NZ, NYL, 16, 128), bf16),
        ]
        + semaphores,
        compiler_params=pltpu.CompilerParams(
            collective_id=0, has_side_effects=True, vmem_limit_bytes=60 << 20
        ),
        cost_estimate=pl.CostEstimate(flops=2_750_000_000, bytes_accessed=8_000_000, transcendentals=524288),
        name="head_loss",
    )(features, proj_weight, texts)
    return grad_features, grad_weight.astype(f32)


def solution(mesh):
    return jax.shard_map(
        shards,
        mesh=mesh,
        in_specs=(P("dp", "mp"), P("mp", None), P(("dp", "mp"), None)),
        out_specs=(P("dp", "mp"), P("mp", None)),
        check_vma=False,
    )
```

```python
import jax
import jax.numpy as jnp
from jax import lax
from jax.experimental import pallas as pl
from jax.experimental.pallas import tpu as pltpu
from jax.sharding import PartitionSpec as P

logit_scale = 100.0
logit_bias = -10.0
epsilon = 1e-06
NX, NYL, NZ = 4, 4, 8
NY = 2 * NYL
MESH = pl.DeviceIdType.MESH
NT = (((1,), (1,)), ((), ()))


def place(x, y, z, c):
    return ((y % NYL) * NX + x) * NZ + z, (y // NYL) * 2 + c


def unit_scale(values):
    return lax.rsqrt(jnp.sum(values * values, axis=1, keepdims=True) + epsilon)


def tile_slots():
    slots = []
    for i in range(6):
        for j in range(9):
            q = i * 9 + j
            slots.append((i, j, q % NX, (q // NX) % NZ, q // (NX * NZ)))
    return slots


def remote(src, dst, s, r, to):
    copy = pltpu.make_async_remote_copy(
        src_ref=src, dst_ref=dst, send_sem=s, recv_sem=r, device_id=to, device_id_type=MESH
    )
    copy.start()
    return copy


def wait_all(copies):
    for copy in copies:
        copy.wait()


HERE = 2


def share(at, ring, to, s, r):
    def go(index, k):
        return remote(at(HERE, None), at((HERE - k) % ring, None), s.at[index], r.at[index], to(k % ring))

    return [go(0, 2), go(1, -2), go(2, 1), go(3, -1)]


def pass_on(at, ring, to, s, r, copies):
    copies[0].wait_recv()
    on = [
        remote(at(0, None), at(7, None), s.at[4], r.at[4], to(1)),
        remote(at(0, 0), at(6, 0), s.at[5], r.at[5], to(2)),
    ]
    copies[1].wait_recv()
    on += [
        remote(at(4, None), at(5, None), s.at[6], r.at[6], to(ring - 1)),
        remote(at(4, 1), at(6, 1), s.at[7], r.at[7], to(ring - 2)),
    ]
    return on


def near(copies):
    copies[2].wait()
    copies[3].wait()


def relay(step, at, ring, to, s, r, before):
    copies = {}
    for piece in range(2):
        for way, d in enumerate((1, -1)):
            if step == 4 and piece != way:
                continue
            if step > 1:
                before[piece, way].wait_recv()
            block = (HERE - d * (step - 1)) % ring
            index = ((step - 1) * 2 + piece) * 2 + way
            copies[piece, way] = remote(
                at(block, piece), at((block - d) % ring, piece), s.at[index], r.at[index], to(d % ring)
            )
    return copies


def finish(copies, on):
    copies[0].wait_send()
    copies[1].wait_send()
    wait_all(on)


def kernel(
    feat_hbm, w_hbm, text_hbm, gfeat_ref, gweight_ref,
    feat, w, text_in, txa, txb, sums, cols, nt_send, nt, part, part_core, part_far, unit, img,
    grad, gs, g_three, g_four, g_one, g_sum, g_two, gproj, wsend, wx, zsend, wz, fin_y, fin_a, fin_b,
    in_s, ax_s, ax_r, az_s, az_r, bx_s, bx_r, bz_s, bz_r, ts_s, ts_r,
    su_s, su_r, co_s, co_r, nt_s, nt_r, pc_s, pc_r, im_s, im_r,
    gy_s, gy_r, gp_s, gp_r, gc_s, gc_r, wx_s, wx_r, wz_s, wz_r, fy_s, fy_r,
    fax_s, fax_r, faz_s, faz_r, fbx_s, fbx_r, fbz_s, fbz_r,
):
    dp = lax.axis_index("dp")
    mp = lax.axis_index("mp")
    yl = dp // (NX * NZ)
    x = (dp // NZ) % NX
    z = dp % NZ
    yh = mp // 2
    c = mp % 2
    y = yh * NYL + yl
    sib = place(x, y, z, 1 - c)
    y_far = (y + NYL) % NY
    far = place(x, y_far, z, c)
    far_sib = place(x, y_far, z, 1 - c)

    def on_y(k):
        return place(x, (y + k) % NY, z, c)

    def on_yl(k):
        return place(x, yh * NYL + (yl + k) % NYL, z, c)

    def on_x(k):
        return place((x + k) % NX, y, z, c)

    def on_z(k):
        return place(x, y, (z + k) % NZ, c)

    barrier = pltpu.get_barrier_semaphore()
    others = [sib, far_sib]
    others += [on_y(k) for k in range(1, NY)]
    others += [on_x(k) for k in range(1, NX)]
    others += [on_z(k) for k in range(1, NZ)]
    for other in others:
        pl.semaphore_signal(barrier, inc=1, device_id=other, device_id_type=MESH)

    text_load = pltpu.make_async_copy(text_hbm, text_in, in_s.at[0])
    feat_load = pltpu.make_async_copy(feat_hbm, feat, in_s.at[1])
    w_load = pltpu.make_async_copy(w_hbm, w, in_s.at[2])
    feat_load.start()
    w_load.start()
    text_load.start()

    e = w.shape[1]
    feat_load.wait()
    inputs = feat[...].astype(jnp.float32)
    row_sum = jnp.broadcast_to(jnp.sum(inputs, axis=1, keepdims=True), (128, 128))
    sums[mp] = row_sum.T[:8]
    w_load.wait()
    partial = jnp.dot(feat[...], w[...], preferred_element_type=jnp.float32)
    for h in range(2):
        for b in range(2):
            lo = (h * 2 + b) * 32
            part[b, h, :, :e] = partial[lo : lo + 32]
            part[b, h, :, e:] = row_sum[lo : lo + 32]
    cols[mp] = jnp.sum(w[...].astype(jnp.float32), axis=0, keepdims=True)
    text_load.wait()
    text = text_in[...].astype(jnp.float32)
    own_text = (text * unit_scale(text)).astype(jnp.bfloat16)
    txa[c, HERE, x] = own_text[:16]
    txb[c, x, HERE] = own_text[16:]
    pl.semaphore_wait(barrier, len(others))

    core_copy = remote(part.at[1 - c], part_core, pc_s.at[0], pc_r.at[0], sib)
    mates = [sib, far, far_sib]
    col_copies = [remote(cols.at[mp], cols.at[mp], co_s.at[k], co_r.at[k], to) for k, to in enumerate(mates)]

    own_a = txa.at[c, HERE, x]
    a_x = [remote(own_a, own_a, ax_s.at[k - 1], ax_r.at[k - 1], on_x(k)) for k in range(1, NX)]

    def a_at(r, half):
        return txa.at[c, r] if half is None else txa.at[c, r, pl.ds(half * (NX // 2), NX // 2)]

    def b_at(r, half):
        if half is None:
            return txb.at[c, x, r]
        return txb.at[c, x, r, :, pl.ds(0, 640)] if half == 0 else txb.at[c, x, r, :, pl.ds(640, 512)]

    def b_to_x(lo, count, index):
        block = txb.at[c, x, pl.ds(lo, count)]
        return [
            remote(block, block, bx_s.at[index + k - 1], bx_r.at[index + k - 1], on_x(k)) for k in range(1, NX)
        ]

    def to_sib(block, index):
        return remote(block, block, ts_s.at[index], ts_r.at[index], sib)

    b_z = share(b_at, NZ, on_z, bz_s, bz_r)

    sum_copies = [remote(sums.at[mp], sums.at[mp], su_s.at[k], su_r.at[k], to) for k, to in enumerate(mates)]

    core_copy.wait()
    part[c, 1 - yh] += part_core[1 - yh]
    far_copy = remote(part.at[c, 1 - yh], part_far, pc_s.at[1], pc_r.at[1], far)
    wait_all(a_x)
    a_1 = relay(1, a_at, NZ, on_z, az_s, az_r, None)
    b_on = pass_on(b_at, NZ, on_z, bz_s, bz_r, b_z)
    near(b_z)
    b_x = b_to_x(0, 5, 0)
    a_2 = relay(2, a_at, NZ, on_z, az_s, az_r, a_1)
    wait_all(col_copies)
    col = (cols[0] + cols[1]) + (cols[2] + cols[3])
    far_copy.wait()
    joined = part[c, yh] + part_core[yh] + part_far[...]
    project = joined[:, :e] - (joined[:, e : e + 1] / 1536.0) * col
    inv_norm = unit_scale(project)
    unit_img = project * inv_norm
    unit[...] = unit_img
    img[HERE] = unit_img.astype(jnp.bfloat16)

    def img_at(r, half):
        return img.at[r] if half is None else img.at[r, pl.ds(half * 16, 16)]

    img_one = share(img_at, NY, on_y, im_s, im_r)
    finish(b_z, b_on)
    b_x2 = b_to_x(5, 3, 3)
    a_3 = relay(3, a_at, NZ, on_z, az_s, az_r, a_2)
    img_on = pass_on(img_at, NY, on_y, im_s, im_r, img_one)
    wait_all(sum_copies)
    total = (sums[0] + sums[1]) + (sums[2] + sums[3])
    mean_in = jnp.broadcast_to(total[:1] / 1536.0, (128, 128)).T[:, :1]
    turned = (feat[...].astype(jnp.float32) - mean_in).T.astype(jnp.bfloat16)
    for g in range(NYL):
        nt_send[g] = turned[g * 96 : (g + 1) * 96]
    nt[yl] = nt_send[yl]
    to_core = [to_sib(txa.at[c, pl.ds(0, 5)], 0)]
    a_4 = relay(4, a_at, NZ, on_z, az_s, az_r, a_3)
    wait_all(b_x)
    to_core += [to_sib(txb.at[c, :, pl.ds(0, 5)], 1)]
    a_3[1, 0].wait_recv()
    a_3[0, 1].wait_recv()
    to_core += [to_sib(txa.at[c, 5], 2), to_sib(txa.at[c, 7], 4)]
    near(img_one)
    finish(img_one, img_on)
    wait_all(b_x2)
    to_core += [to_sib(txb.at[c, :, pl.ds(5, 3)], 3)]
    for copies in (a_1, a_2, a_3, a_4):
        for copy in copies.values():
            copy.wait_send()
    for copy in a_4.values():
        copy.wait_recv()
    to_core += [to_sib(txa.at[c, 6], 5)]
    nt_copies = [
        remote(nt_send.at[(yl + k) % NYL], nt.at[yl], nt_s.at[k - 1], nt_r.at[k - 1], on_yl(k))
        for k in range(1, NYL)
    ]

    def add_texts(block, first):
        texts = block[...].reshape(NX * NZ * 16, -1)
        images = img[...].reshape(NY * 32, -1)
        score = lax.dot_general(images, texts, NT, preferred_element_type=jnp.float32)
        slope = jax.nn.sigmoid(logit_scale * score + logit_bias).astype(jnp.bfloat16)
        terms = jnp.dot(slope, texts, preferred_element_type=jnp.float32).reshape(grad.shape)
        grad[...] = terms if first else grad[...] + terms

    add_texts(txa.at[c], True)
    add_texts(txb.at[c], False)
    wait_all(to_core)
    add_texts(txa.at[1 - c], False)
    add_texts(txb.at[1 - c], False)

    for r in (5, 7, 6, 3, 1):
        gs[r] = grad[r].astype(jnp.bfloat16)

    def give(src, dst, index, k):
        return remote(src, dst, gy_s.at[index], gy_r.at[index], on_y(k))

    three = [give(gs.at[5], g_three.at[0], 0, 1), give(gs.at[7], g_three.at[1], 1, NY - 1)]
    four = [
        give(gs.at[6, pl.ds(0, 16)], g_four.at[0], 2, 2),
        give(gs.at[6, pl.ds(16, 16)], g_four.at[1], 3, NY - 2),
    ]
    one = [give(gs.at[3], g_one.at[0], 4, 1), give(gs.at[1], g_one.at[1], 5, NY - 1)]
    own_b16 = img[HERE].astype(jnp.float32)
    own_t = jnp.concatenate([txa[c, HERE, x], txb[c, x, HERE]], axis=0).astype(jnp.float32)
    own_logit = logit_scale * jnp.sum(own_b16 * own_t, axis=1, keepdims=True) + logit_bias
    wrong = jax.nn.sigmoid(own_logit).astype(jnp.bfloat16).astype(jnp.float32)
    right = (-jax.nn.sigmoid(-own_logit)).astype(jnp.bfloat16).astype(jnp.float32)
    grad_unit = grad[HERE] + (right - wrong) * own_t
    wsend[...] = jnp.zeros_like(wsend)
    two = []
    for side, k in ((0, 2), (1, NY - 2)):
        three[side].wait()
        four[side].wait()
        far_sum = grad[(HERE + k) % NY] + g_three[side].astype(jnp.float32)
        lo, hi = far_sum[:16], far_sum[16:]
        if side == 0:
            lo = lo + g_four[0].astype(jnp.float32)
        else:
            hi = hi + g_four[1].astype(jnp.float32)
        g_sum[side, :16] = lo.astype(jnp.bfloat16)
        g_sum[side, 16:] = hi.astype(jnp.bfloat16)
        two.append(give(g_sum.at[side], g_two.at[side], 6 + side, k))
    wait_all(one + two)
    for side in range(2):
        grad_unit = grad_unit + g_one[side].astype(jnp.float32) + g_two[side].astype(jnp.float32)
    grad_unit = logit_scale * grad_unit
    unit_img = unit[...]
    along = jnp.sum(unit_img * grad_unit, axis=1, keepdims=True)
    gproj[c, HERE] = (inv_norm * (grad_unit - unit_img * along)).astype(jnp.bfloat16)

    def gp_at(r, half):
        return gproj.at[c, r] if half is None else gproj.at[c, r, pl.ds(half * 16, 16)]

    def gp_to_sib(lo, count, index):
        block = gproj.at[c, pl.ds(lo, count)]
        return remote(block, block, gc_s.at[index], gc_r.at[index], sib)

    gp_one = share(gp_at, NY, on_y, gp_s, gp_r)
    wait_all(nt_copies)
    gp_on = pass_on(gp_at, NY, on_y, gp_s, gp_r, gp_one)
    near(gp_one)
    gp_core = [gp_to_sib(0, 5, 0)]
    finish(gp_one, gp_on)
    gp_core += [gp_to_sib(5, 3, 1)]
    wait_all(gp_core)

    def group_rows(g):
        low, high = (g - y + HERE + NY) % NY, (g - y + HERE + NY + NYL) % NY
        return jnp.concatenate([gproj[0, low], gproj[1, low], gproj[0, high], gproj[1, high]], axis=0)

    weight_part = jnp.dot(nt[0], group_rows(0), preferred_element_type=jnp.float32)
    for g in range(1, NYL):
        weight_part += jnp.dot(nt[g], group_rows(g), preferred_element_type=jnp.float32)
    weight_part = weight_part.astype(jnp.bfloat16)
    slots = tile_slots()
    for i, j, tx, tz, k in slots:
        wsend[tx, tz, k] = weight_part[i * 16 : (i + 1) * 16, j * 128 : (j + 1) * 128]
    wx_copies = [
        remote(wsend.at[(x + k) % NX], wx.at[x], wx_s.at[k - 1], wx_r.at[k - 1], on_x(k)) for k in range(1, NX)
    ]
    wx[x] = wsend[x]
    rows = group_rows(yl)
    grad_normed = lax.dot_general(rows, w[...], NT, preferred_element_type=jnp.float32)
    grad_total = jnp.sum(rows.astype(jnp.float32) * col, axis=1, keepdims=True)
    gfeat_ref[...] = (grad_normed - grad_total / 1536.0).astype(jnp.bfloat16)
    wait_all(wx_copies)
    over_x = wx[0].astype(jnp.float32)
    for k in range(1, NX):
        over_x += wx[k].astype(jnp.float32)
    zsend[...] = over_x.astype(jnp.bfloat16)
    wz_copies = [
        remote(zsend.at[(z + k) % NZ], wz.at[z], wz_s.at[k - 1], wz_r.at[k - 1], on_z(k)) for k in range(1, NZ)
    ]
    wz[z] = zsend[z]
    wait_all(wz_copies)
    over_z = wz[0].astype(jnp.float32)
    for k in range(1, NZ):
        over_z += wz[k].astype(jnp.float32)
    fin_y[yl] = over_z.astype(jnp.bfloat16)
    wait_all(
        [remote(fin_y.at[yl], fin_y.at[yl], fy_s.at[k - 1], fy_r.at[k - 1], on_yl(k)) for k in range(1, NYL)]
    )
    fin_a[HERE, x] = fin_y[:, 0]
    fin_b[x, HERE] = fin_y[:, 1]
    own_fa = fin_a.at[HERE, x]
    fa_x = [remote(own_fa, own_fa, fax_s.at[k - 1], fax_r.at[k - 1], on_x(k)) for k in range(1, NX)]

    def fa_at(r, half):
        return fin_a.at[r] if half is None else fin_a.at[r, pl.ds(half * (NX // 2), NX // 2)]

    def fb_at(r, half):
        return fin_b.at[x, r] if half is None else fin_b.at[x, r, pl.ds(half * (NYL // 2), NYL // 2)]

    def fb_to_x(lo, count, index):
        block = fin_b.at[x, pl.ds(lo, count)]
        return [
            remote(block, block, fbx_s.at[index + k - 1], fbx_r.at[index + k - 1], on_x(k)) for k in range(1, NX)
        ]

    fb_z = share(fb_at, NZ, on_z, fbz_s, fbz_r)
    wait_all(fa_x)
    fa_z = share(fa_at, NZ, on_z, faz_s, faz_r)
    fb_on = pass_on(fb_at, NZ, on_z, fbz_s, fbz_r, fb_z)
    near(fb_z)
    fb_x = fb_to_x(0, 5, 0)
    fa_on = pass_on(fa_at, NZ, on_z, faz_s, faz_r, fa_z)
    finish(fb_z, fb_on)
    fb_x += fb_to_x(5, 3, 3)
    near(fa_z)
    finish(fa_z, fa_on)
    wait_all(fb_x)
    at_z = [(tz - z + HERE + NZ) % NZ for tz in range(NZ)]
    for g in range(NYL):
        for i, j, tx, tz, k in slots:
            tile = fin_a[at_z[tz], tx, g] if k == 0 else fin_b[tx, at_z[tz], g]
            gweight_ref[g * 96 + i * 16 : g * 96 + (i + 1) * 16, j * 128 : (j + 1) * 128] = tile


def shards(features, proj_weight, texts):
    rows, width = features.shape
    e = proj_weight.shape[1]
    bf16, f32 = jnp.bfloat16, jnp.float32
    dma = pltpu.SemaphoreType.DMA
    counts = [3, 16, 6, 8, 6, 3, 3, NYL - 1, 2, 8, 8, 8, 2, NX - 1, NZ - 1, NYL - 1, 3, 8, 6, 8]
    semaphores = [dma((3,))] + [dma((n,)) for n in counts for _ in range(2)]
    hbm = pl.BlockSpec(memory_space=pltpu.HBM)
    grad_features, grad_weight = pl.pallas_call(
        kernel,
        out_shape=(
            jax.ShapeDtypeStruct((rows, width), bf16),
            jax.ShapeDtypeStruct((width, e), bf16),
        ),
        in_specs=[hbm] * 3,
        out_specs=[pl.BlockSpec(memory_space=pltpu.VMEM)] * 2,
        scratch_shapes=[
            pltpu.VMEM((rows, width), bf16),
            pltpu.VMEM((width, e), bf16),
            pltpu.VMEM((32, e), bf16),
            pltpu.VMEM((2, NZ, NX, 16, e), bf16),
            pltpu.VMEM((2, NX, NZ, 16, e), bf16),
            pltpu.VMEM((4, 8, 128), f32),
            pltpu.VMEM((4, 1, e), f32),
            pltpu.VMEM((NYL, width // NYL, rows), bf16),
            pltpu.VMEM((NYL, width // NYL, rows), bf16),
            pltpu.VMEM((2, 2, 32, e + 128), f32),
            pltpu.VMEM((2, 32, e + 128), f32),
            pltpu.VMEM((32, e + 128), f32),
            pltpu.VMEM((32, e), f32),
            pltpu.VMEM((NY, 32, e), bf16),
            pltpu.VMEM((NY, 32, e), f32),
            pltpu.VMEM((NY, 32, e), bf16),
            pltpu.VMEM((2, 32, e), bf16),
            pltpu.VMEM((2, 16, e), bf16),
            pltpu.VMEM((2, 32, e), bf16),
            pltpu.VMEM((2, 32, e), bf16),
            pltpu.VMEM((2, 32, e), bf16),
            pltpu.VMEM((2, NY, 32, e), bf16),
            pltpu.VMEM((NX, NZ, 2, 16, 128), bf16),
            pltpu.VMEM((NX, NZ, 2, 16, 128), bf16),
            pltpu.VMEM((NZ, 2, 16, 128), bf16),
            pltpu.VMEM((NZ, 2, 16, 128), bf16),
            pltpu.VMEM((NYL, 2, 16, 128), bf16),
            pltpu.VMEM((NZ, NX, NYL, 16, 128), bf16),
            pltpu.VMEM((NX, NZ, NYL, 16, 128), bf16),
        ]
        + semaphores,
        compiler_params=pltpu.CompilerParams(
            collective_id=0, has_side_effects=True, vmem_limit_bytes=60 << 20
        ),
        cost_estimate=pl.CostEstimate(flops=2_750_000_000, bytes_accessed=8_000_000, transcendentals=524288),
        name="head_loss",
    )(features, proj_weight, texts)
    return grad_features, grad_weight.astype(f32)


def solution(mesh):
    return jax.shard_map(
        shards,
        mesh=mesh,
        in_specs=(P("dp", "mp"), P("mp", None), P(("dp", "mp"), None)),
        out_specs=(P("dp", "mp"), P("mp", None)),
        check_vma=False,
    )
```

```python
import jax
import jax.numpy as jnp
from jax import lax
from jax.experimental import pallas as pl
from jax.experimental.pallas import tpu as pltpu
from jax.sharding import PartitionSpec as P

logit_scale = 100.0
logit_bias = -10.0
epsilon = 1e-06
NX, NYL, NZ = 4, 4, 8
NY = 2 * NYL
MESH = pl.DeviceIdType.MESH
NT = (((1,), (1,)), ((), ()))


def place(x, y, z, c):
    return ((y % NYL) * NX + x) * NZ + z, (y // NYL) * 2 + c


def unit_scale(values):
    return lax.rsqrt(jnp.sum(values * values, axis=1, keepdims=True) + epsilon)


def tile_slots():
    slots = []
    for i in range(6):
        for j in range(9):
            q = i * 9 + j
            slots.append((i, j, q % NX, (q // NX) % NZ, q // (NX * NZ)))
    return slots


def remote(src, dst, s, r, to):
    copy = pltpu.make_async_remote_copy(
        src_ref=src, dst_ref=dst, send_sem=s, recv_sem=r, device_id=to, device_id_type=MESH
    )
    copy.start()
    return copy


def wait_all(copies):
    for copy in copies:
        copy.wait()


HERE = 2


def share(at, ring, to, s, r):
    def go(index, k):
        return remote(at(HERE, None), at((HERE - k) % ring, None), s.at[index], r.at[index], to(k % ring))

    return [go(0, 2), go(1, -2), go(2, 1), go(3, -1)]


def pass_on(at, ring, to, s, r, copies):
    copies[0].wait_recv()
    on = [
        remote(at(0, None), at(7, None), s.at[4], r.at[4], to(1)),
        remote(at(0, 0), at(6, 0), s.at[5], r.at[5], to(2)),
    ]
    copies[1].wait_recv()
    on += [
        remote(at(4, None), at(5, None), s.at[6], r.at[6], to(ring - 1)),
        remote(at(4, 1), at(6, 1), s.at[7], r.at[7], to(ring - 2)),
    ]
    return on


def near(copies):
    copies[2].wait()
    copies[3].wait()


def relay(step, at, ring, to, s, r, before):
    copies = {}
    for piece in range(2):
        for way, d in enumerate((1, -1)):
            if step == 4 and piece != way:
                continue
            if step > 1:
                before[piece, way].wait_recv()
            block = (HERE - d * (step - 1)) % ring
            index = ((step - 1) * 2 + piece) * 2 + way
            copies[piece, way] = remote(
                at(block, piece), at((block - d) % ring, piece), s.at[index], r.at[index], to(d % ring)
            )
    return copies


def finish(copies, on):
    copies[0].wait_send()
    copies[1].wait_send()
    wait_all(on)


def kernel(
    feat_hbm, w_hbm, text_hbm, gfeat_ref, gweight_ref,
    feat, w, text_in, txa, txb, sums, cols, nt_send, nt, part, part_core, part_far, unit, img,
    grad, gs, g_three, g_four, g_one, g_sum, g_two, gproj, wsend, wx, zsend, wz, fin_a, fin_b,
    in_s, ax_s, ax_r, az_s, az_r, bx_s, bx_r, bz_s, bz_r, ts_s, ts_r,
    su_s, su_r, co_s, co_r, nt_s, nt_r, pc_s, pc_r, im_s, im_r,
    gy_s, gy_r, gp_s, gp_r, gc_s, gc_r, wx_s, wx_r, wz_s, wz_r, fy_s, fy_r,
    fax_s, fax_r, faz_s, faz_r, fbx_s, fbx_r, fbz_s, fbz_r,
):
    dp = lax.axis_index("dp")
    mp = lax.axis_index("mp")
    yl = dp // (NX * NZ)
    x = (dp // NZ) % NX
    z = dp % NZ
    yh = mp // 2
    c = mp % 2
    y = yh * NYL + yl
    sib = place(x, y, z, 1 - c)
    y_far = (y + NYL) % NY
    far = place(x, y_far, z, c)
    far_sib = place(x, y_far, z, 1 - c)

    def on_y(k):
        return place(x, (y + k) % NY, z, c)

    def on_yl(k):
        return place(x, yh * NYL + (yl + k) % NYL, z, c)

    def on_x(k):
        return place((x + k) % NX, y, z, c)

    def on_yl_x(j, k):
        return place((x + k) % NX, yh * NYL + (yl + j) % NYL, z, c)

    def on_z(k):
        return place(x, y, (z + k) % NZ, c)

    barrier = pltpu.get_barrier_semaphore()
    others = [sib, far_sib]
    others += [on_y(k) for k in range(1, NY)]
    others += [on_x(k) for k in range(1, NX)]
    others += [on_z(k) for k in range(1, NZ)]
    others += [on_yl_x(j, k) for j in range(1, NYL) for k in range(1, NX)]
    for other in others:
        pl.semaphore_signal(barrier, inc=1, device_id=other, device_id_type=MESH)

    text_load = pltpu.make_async_copy(text_hbm, text_in, in_s.at[0])
    feat_load = pltpu.make_async_copy(feat_hbm, feat, in_s.at[1])
    w_load = pltpu.make_async_copy(w_hbm, w, in_s.at[2])
    feat_load.start()
    w_load.start()
    text_load.start()

    e = w.shape[1]
    feat_load.wait()
    inputs = feat[...].astype(jnp.float32)
    row_sum = jnp.broadcast_to(jnp.sum(inputs, axis=1, keepdims=True), (128, 128))
    sums[mp] = row_sum.T[:8]
    w_load.wait()
    partial = jnp.dot(feat[...], w[...], preferred_element_type=jnp.float32)
    for h in range(2):
        for b in range(2):
            lo = (h * 2 + b) * 32
            part[b, h, :, :e] = partial[lo : lo + 32]
            part[b, h, :, e:] = row_sum[lo : lo + 32]
    cols[mp] = jnp.sum(w[...].astype(jnp.float32), axis=0, keepdims=True)
    text_load.wait()
    text = text_in[...].astype(jnp.float32)
    own_text = (text * unit_scale(text)).astype(jnp.bfloat16)
    txa[c, HERE, x] = own_text[:16]
    txb[c, x, HERE] = own_text[16:]
    pl.semaphore_wait(barrier, len(others))

    core_copy = remote(part.at[1 - c], part_core, pc_s.at[0], pc_r.at[0], sib)
    mates = [sib, far, far_sib]
    col_copies = [remote(cols.at[mp], cols.at[mp], co_s.at[k], co_r.at[k], to) for k, to in enumerate(mates)]

    own_a = txa.at[c, HERE, x]
    a_x = [remote(own_a, own_a, ax_s.at[k - 1], ax_r.at[k - 1], on_x(k)) for k in range(1, NX)]

    def a_at(r, half):
        return txa.at[c, r] if half is None else txa.at[c, r, pl.ds(half * (NX // 2), NX // 2)]

    def b_at(r, half):
        if half is None:
            return txb.at[c, x, r]
        return txb.at[c, x, r, :, pl.ds(0, 640)] if half == 0 else txb.at[c, x, r, :, pl.ds(640, 512)]

    def b_to_x(lo, count, index):
        block = txb.at[c, x, pl.ds(lo, count)]
        return [
            remote(block, block, bx_s.at[index + k - 1], bx_r.at[index + k - 1], on_x(k)) for k in range(1, NX)
        ]

    def to_sib(block, index):
        return remote(block, block, ts_s.at[index], ts_r.at[index], sib)

    b_z = share(b_at, NZ, on_z, bz_s, bz_r)

    sum_copies = [remote(sums.at[mp], sums.at[mp], su_s.at[k], su_r.at[k], to) for k, to in enumerate(mates)]

    core_copy.wait()
    part[c, 1 - yh] += part_core[1 - yh]
    far_copy = remote(part.at[c, 1 - yh], part_far, pc_s.at[1], pc_r.at[1], far)
    wait_all(a_x)
    a_1 = relay(1, a_at, NZ, on_z, az_s, az_r, None)
    b_on = pass_on(b_at, NZ, on_z, bz_s, bz_r, b_z)
    near(b_z)
    b_x = b_to_x(0, 5, 0)
    a_2 = relay(2, a_at, NZ, on_z, az_s, az_r, a_1)
    wait_all(col_copies)
    col = (cols[0] + cols[1]) + (cols[2] + cols[3])
    far_copy.wait()
    joined = part[c, yh] + part_core[yh] + part_far[...]
    project = joined[:, :e] - (joined[:, e : e + 1] / 1536.0) * col
    inv_norm = unit_scale(project)
    unit_img = project * inv_norm
    unit[...] = unit_img
    img[HERE] = unit_img.astype(jnp.bfloat16)

    def img_at(r, half):
        return img.at[r] if half is None else img.at[r, pl.ds(half * 16, 16)]

    img_one = share(img_at, NY, on_y, im_s, im_r)
    finish(b_z, b_on)
    b_x2 = b_to_x(5, 3, 3)
    a_3 = relay(3, a_at, NZ, on_z, az_s, az_r, a_2)
    img_on = pass_on(img_at, NY, on_y, im_s, im_r, img_one)
    wait_all(sum_copies)
    total = (sums[0] + sums[1]) + (sums[2] + sums[3])
    mean_in = jnp.broadcast_to(total[:1] / 1536.0, (128, 128)).T[:, :1]
    turned = (feat[...].astype(jnp.float32) - mean_in).T.astype(jnp.bfloat16)
    for g in range(NYL):
        nt_send[g] = turned[g * 96 : (g + 1) * 96]
    nt[yl] = nt_send[yl]
    to_core = [to_sib(txa.at[c, pl.ds(0, 5)], 0)]
    a_4 = relay(4, a_at, NZ, on_z, az_s, az_r, a_3)
    wait_all(b_x)
    to_core += [to_sib(txb.at[c, :, pl.ds(0, 5)], 1)]
    a_3[1, 0].wait_recv()
    a_3[0, 1].wait_recv()
    to_core += [to_sib(txa.at[c, 5], 2), to_sib(txa.at[c, 7], 4)]
    near(img_one)
    finish(img_one, img_on)
    wait_all(b_x2)
    to_core += [to_sib(txb.at[c, :, pl.ds(5, 3)], 3)]
    for copies in (a_1, a_2, a_3, a_4):
        for copy in copies.values():
            copy.wait_send()
    for copy in a_4.values():
        copy.wait_recv()
    to_core += [to_sib(txa.at[c, 6], 5)]
    nt_copies = [
        remote(nt_send.at[(yl + k) % NYL], nt.at[yl], nt_s.at[k - 1], nt_r.at[k - 1], on_yl(k))
        for k in range(1, NYL)
    ]

    def add_texts(block, first):
        texts = block[...].reshape(NX * NZ * 16, -1)
        images = img[...].reshape(NY * 32, -1)
        score = lax.dot_general(images, texts, NT, preferred_element_type=jnp.float32)
        slope = jax.nn.sigmoid(logit_scale * score + logit_bias).astype(jnp.bfloat16)
        terms = jnp.dot(slope, texts, preferred_element_type=jnp.float32).reshape(grad.shape)
        grad[...] = terms if first else grad[...] + terms

    add_texts(txa.at[c], True)
    add_texts(txb.at[c], False)
    wait_all(to_core)
    add_texts(txa.at[1 - c], False)
    add_texts(txb.at[1 - c], False)

    for r in (5, 7, 6, 3, 1):
        gs[r] = grad[r].astype(jnp.bfloat16)

    def give(src, dst, index, k):
        return remote(src, dst, gy_s.at[index], gy_r.at[index], on_y(k))

    three = [give(gs.at[5], g_three.at[0], 0, 1), give(gs.at[7], g_three.at[1], 1, NY - 1)]
    four = [
        give(gs.at[6, pl.ds(0, 16)], g_four.at[0], 2, 2),
        give(gs.at[6, pl.ds(16, 16)], g_four.at[1], 3, NY - 2),
    ]
    one = [give(gs.at[3], g_one.at[0], 4, 1), give(gs.at[1], g_one.at[1], 5, NY - 1)]
    own_b16 = img[HERE].astype(jnp.float32)
    own_t = jnp.concatenate([txa[c, HERE, x], txb[c, x, HERE]], axis=0).astype(jnp.float32)
    own_logit = logit_scale * jnp.sum(own_b16 * own_t, axis=1, keepdims=True) + logit_bias
    wrong = jax.nn.sigmoid(own_logit).astype(jnp.bfloat16).astype(jnp.float32)
    right = (-jax.nn.sigmoid(-own_logit)).astype(jnp.bfloat16).astype(jnp.float32)
    grad_unit = grad[HERE] + (right - wrong) * own_t
    wsend[...] = jnp.zeros_like(wsend)
    two = []
    for side, k in ((0, 2), (1, NY - 2)):
        three[side].wait()
        four[side].wait()
        far_sum = grad[(HERE + k) % NY] + g_three[side].astype(jnp.float32)
        lo, hi = far_sum[:16], far_sum[16:]
        if side == 0:
            lo = lo + g_four[0].astype(jnp.float32)
        else:
            hi = hi + g_four[1].astype(jnp.float32)
        g_sum[side, :16] = lo.astype(jnp.bfloat16)
        g_sum[side, 16:] = hi.astype(jnp.bfloat16)
        two.append(give(g_sum.at[side], g_two.at[side], 6 + side, k))
    wait_all(one + two)
    for side in range(2):
        grad_unit = grad_unit + g_one[side].astype(jnp.float32) + g_two[side].astype(jnp.float32)
    grad_unit = logit_scale * grad_unit
    unit_img = unit[...]
    along = jnp.sum(unit_img * grad_unit, axis=1, keepdims=True)
    gproj[c, HERE] = (inv_norm * (grad_unit - unit_img * along)).astype(jnp.bfloat16)

    def gp_at(r, half):
        return gproj.at[c, r] if half is None else gproj.at[c, r, pl.ds(half * 16, 16)]

    def gp_to_sib(lo, count, index):
        block = gproj.at[c, pl.ds(lo, count)]
        return remote(block, block, gc_s.at[index], gc_r.at[index], sib)

    gp_one = share(gp_at, NY, on_y, gp_s, gp_r)
    wait_all(nt_copies)
    gp_on = pass_on(gp_at, NY, on_y, gp_s, gp_r, gp_one)
    near(gp_one)
    gp_core = [gp_to_sib(0, 5, 0)]
    finish(gp_one, gp_on)
    gp_core += [gp_to_sib(5, 3, 1)]
    wait_all(gp_core)

    def group_rows(g):
        low, high = (g - y + HERE + NY) % NY, (g - y + HERE + NY + NYL) % NY
        return jnp.concatenate([gproj[0, low], gproj[1, low], gproj[0, high], gproj[1, high]], axis=0)

    weight_part = jnp.dot(nt[0], group_rows(0), preferred_element_type=jnp.float32)
    for g in range(1, NYL):
        weight_part += jnp.dot(nt[g], group_rows(g), preferred_element_type=jnp.float32)
    weight_part = weight_part.astype(jnp.bfloat16)
    slots = tile_slots()
    for i, j, tx, tz, k in slots:
        wsend[tx, tz, k] = weight_part[i * 16 : (i + 1) * 16, j * 128 : (j + 1) * 128]
    wx_copies = [
        remote(wsend.at[(x + k) % NX], wx.at[x], wx_s.at[k - 1], wx_r.at[k - 1], on_x(k)) for k in range(1, NX)
    ]
    wx[x] = wsend[x]
    rows = group_rows(yl)
    grad_normed = lax.dot_general(rows, w[...], NT, preferred_element_type=jnp.float32)
    grad_total = jnp.sum(rows.astype(jnp.float32) * col, axis=1, keepdims=True)
    gfeat_ref[...] = (grad_normed - grad_total / 1536.0).astype(jnp.bfloat16)
    wait_all(wx_copies)
    over_x = wx[0].astype(jnp.float32)
    for k in range(1, NX):
        over_x += wx[k].astype(jnp.float32)
    zsend[...] = over_x.astype(jnp.bfloat16)
    wz_copies = [
        remote(zsend.at[(z + k) % NZ], wz.at[z], wz_s.at[k - 1], wz_r.at[k - 1], on_z(k)) for k in range(1, NZ)
    ]
    wz[z] = zsend[z]
    wait_all(wz_copies)
    over_z = wz[0].astype(jnp.float32)
    for k in range(1, NZ):
        over_z += wz[k].astype(jnp.float32)
    done = over_z.astype(jnp.bfloat16)
    fin_a[HERE, x, yl] = done[0]
    fin_b[x, HERE, yl] = done[1]
    own_fb = fin_b.at[x, HERE, yl]
    fb_y = [remote(own_fb, own_fb, fy_s.at[k - 1], fy_r.at[k - 1], on_yl(k)) for k in range(1, NYL)]
    own_fa = fin_a.at[HERE, x, yl]
    fa_x = [
        remote(own_fa, own_fa, fax_s.at[j * NX + k], fax_r.at[j * NX + k], on_yl_x(j, k))
        for j in range(NYL)
        for k in range(NX)
        if j + k > 0
    ]

    def fa_at(r, half):
        return fin_a.at[r] if half is None else fin_a.at[r, pl.ds(half * (NX // 2), NX // 2)]

    def fb_at(r, half):
        return fin_b.at[x, r] if half is None else fin_b.at[x, r, pl.ds(half * (NYL // 2), NYL // 2)]

    def fb_to_x(lo, count, index):
        block = fin_b.at[x, pl.ds(lo, count)]
        return [
            remote(block, block, fbx_s.at[index + k - 1], fbx_r.at[index + k - 1], on_x(k)) for k in range(1, NX)
        ]

    wait_all(fb_y)
    fb_z = share(fb_at, NZ, on_z, fbz_s, fbz_r)
    wait_all(fa_x)
    fa_z = share(fa_at, NZ, on_z, faz_s, faz_r)
    fb_on = pass_on(fb_at, NZ, on_z, fbz_s, fbz_r, fb_z)
    near(fb_z)
    fb_x = fb_to_x(0, 5, 0)
    fa_on = pass_on(fa_at, NZ, on_z, faz_s, faz_r, fa_z)
    finish(fb_z, fb_on)
    fb_x += fb_to_x(5, 3, 3)
    near(fa_z)
    finish(fa_z, fa_on)
    wait_all(fb_x)
    at_z = [(tz - z + HERE + NZ) % NZ for tz in range(NZ)]
    for g in range(NYL):
        for i, j, tx, tz, k in slots:
            tile = fin_a[at_z[tz], tx, g] if k == 0 else fin_b[tx, at_z[tz], g]
            gweight_ref[g * 96 + i * 16 : g * 96 + (i + 1) * 16, j * 128 : (j + 1) * 128] = tile


def shards(features, proj_weight, texts):
    rows, width = features.shape
    e = proj_weight.shape[1]
    bf16, f32 = jnp.bfloat16, jnp.float32
    dma = pltpu.SemaphoreType.DMA
    counts = [3, 16, 6, 8, 6, 3, 3, NYL - 1, 2, 8, 8, 8, 2, NX - 1, NZ - 1, NYL - 1, NYL * NX, 8, 6, 8]
    semaphores = [dma((3,))] + [dma((n,)) for n in counts for _ in range(2)]
    hbm = pl.BlockSpec(memory_space=pltpu.HBM)
    grad_features, grad_weight = pl.pallas_call(
        kernel,
        out_shape=(
            jax.ShapeDtypeStruct((rows, width), bf16),
            jax.ShapeDtypeStruct((width, e), bf16),
        ),
        in_specs=[hbm] * 3,
        out_specs=[pl.BlockSpec(memory_space=pltpu.VMEM)] * 2,
        scratch_shapes=[
            pltpu.VMEM((rows, width), bf16),
            pltpu.VMEM((width, e), bf16),
            pltpu.VMEM((32, e), bf16),
            pltpu.VMEM((2, NZ, NX, 16, e), bf16),
            pltpu.VMEM((2, NX, NZ, 16, e), bf16),
            pltpu.VMEM((4, 8, 128), f32),
            pltpu.VMEM((4, 1, e), f32),
            pltpu.VMEM((NYL, width // NYL, rows), bf16),
            pltpu.VMEM((NYL, width // NYL, rows), bf16),
            pltpu.VMEM((2, 2, 32, e + 128), f32),
            pltpu.VMEM((2, 32, e + 128), f32),
            pltpu.VMEM((32, e + 128), f32),
            pltpu.VMEM((32, e), f32),
            pltpu.VMEM((NY, 32, e), bf16),
            pltpu.VMEM((NY, 32, e), f32),
            pltpu.VMEM((NY, 32, e), bf16),
            pltpu.VMEM((2, 32, e), bf16),
            pltpu.VMEM((2, 16, e), bf16),
            pltpu.VMEM((2, 32, e), bf16),
            pltpu.VMEM((2, 32, e), bf16),
            pltpu.VMEM((2, 32, e), bf16),
            pltpu.VMEM((2, NY, 32, e), bf16),
            pltpu.VMEM((NX, NZ, 2, 16, 128), bf16),
            pltpu.VMEM((NX, NZ, 2, 16, 128), bf16),
            pltpu.VMEM((NZ, 2, 16, 128), bf16),
            pltpu.VMEM((NZ, 2, 16, 128), bf16),
            pltpu.VMEM((NZ, NX, NYL, 16, 128), bf16),
            pltpu.VMEM((NX, NZ, NYL, 16, 128), bf16),
        ]
        + semaphores,
        compiler_params=pltpu.CompilerParams(
            collective_id=0, has_side_effects=True, vmem_limit_bytes=60 << 20
        ),
        cost_estimate=pl.CostEstimate(flops=2_750_000_000, bytes_accessed=8_000_000, transcendentals=524288),
        name="head_loss",
    )(features, proj_weight, texts)
    return grad_features, grad_weight.astype(f32)


def solution(mesh):
    return jax.shard_map(
        shards,
        mesh=mesh,
        in_specs=(P("dp", "mp"), P("mp", None), P(("dp", "mp"), None)),
        out_specs=(P("dp", "mp"), P("mp", None)),
        check_vma=False,
    )
```

```python
import jax
import jax.numpy as jnp
from jax import lax
from jax.experimental import pallas as pl
from jax.experimental.pallas import tpu as pltpu
from jax.sharding import PartitionSpec as P

logit_scale = 100.0
logit_bias = -10.0
epsilon = 1e-06
NX, NYL, NZ = 4, 4, 8
NY = 2 * NYL
MESH = pl.DeviceIdType.MESH
NT = (((1,), (1,)), ((), ()))


def place(x, y, z, c):
    return ((y % NYL) * NX + x) * NZ + z, (y // NYL) * 2 + c


def unit_scale(values):
    return lax.rsqrt(jnp.sum(values * values, axis=1, keepdims=True) + epsilon)


def tile_slots():
    slots = []
    for i in range(6):
        for j in range(9):
            q = i * 9 + j
            slots.append((i, j, q % NX, (q // NX) % NZ, q // (NX * NZ)))
    return slots


def remote(src, dst, s, r, to):
    copy = pltpu.make_async_remote_copy(
        src_ref=src, dst_ref=dst, send_sem=s, recv_sem=r, device_id=to, device_id_type=MESH
    )
    copy.start()
    return copy


def wait_all(copies):
    for copy in copies:
        copy.wait()


HERE = 2


def share(at, ring, to, s, r):
    def go(index, k):
        return remote(at(HERE, None), at((HERE - k) % ring, None), s.at[index], r.at[index], to(k % ring))

    return [go(0, 2), go(1, -2), go(2, 1), go(3, -1)]


def pass_on(at, ring, to, s, r, copies):
    copies[0].wait_recv()
    on = [
        remote(at(0, None), at(7, None), s.at[4], r.at[4], to(1)),
        remote(at(0, 0), at(6, 0), s.at[5], r.at[5], to(2)),
    ]
    copies[1].wait_recv()
    on += [
        remote(at(4, None), at(5, None), s.at[6], r.at[6], to(ring - 1)),
        remote(at(4, 1), at(6, 1), s.at[7], r.at[7], to(ring - 2)),
    ]
    return on


def near(copies):
    copies[2].wait()
    copies[3].wait()


def relay(step, at, ring, to, s, r, before):
    copies = {}
    for piece in range(2):
        for way, d in enumerate((1, -1)):
            if step == 4 and piece != way:
                continue
            if step > 1:
                before[piece, way].wait_recv()
            block = (HERE - d * (step - 1)) % ring
            index = ((step - 1) * 2 + piece) * 2 + way
            copies[piece, way] = remote(
                at(block, piece), at((block - d) % ring, piece), s.at[index], r.at[index], to(d % ring)
            )
    return copies


def finish(copies, on):
    copies[0].wait_send()
    copies[1].wait_send()
    wait_all(on)


def kernel(
    feat_hbm, w_hbm, text_hbm, gfeat_ref, gweight_ref,
    feat, w, text_in, txa, txb, sums, cols, nt_send, nt, part, part_core, part_far, unit, img,
    grad, gs, g_three, g_four, g_one, g_sum, g_two, gproj, wsend, wx, zsend, wz, fin_a, fin_b,
    in_s, ax_s, ax_r, az_s, az_r, bx_s, bx_r, bz_s, bz_r, ts_s, ts_r,
    su_s, su_r, co_s, co_r, nt_s, nt_r, pc_s, pc_r, im_s, im_r,
    gy_s, gy_r, gp_s, gp_r, gc_s, gc_r, wx_s, wx_r, wz_s, wz_r, fy_s, fy_r,
    fax_s, fax_r, faz_s, faz_r, fbx_s, fbx_r, fbz_s, fbz_r,
):
    dp = lax.axis_index("dp")
    mp = lax.axis_index("mp")
    yl = dp // (NX * NZ)
    x = (dp // NZ) % NX
    z = dp % NZ
    yh = mp // 2
    c = mp % 2
    y = yh * NYL + yl
    sib = place(x, y, z, 1 - c)
    y_far = (y + NYL) % NY
    far = place(x, y_far, z, c)
    far_sib = place(x, y_far, z, 1 - c)

    def on_y(k):
        return place(x, (y + k) % NY, z, c)

    def on_yl(k):
        return place(x, yh * NYL + (yl + k) % NYL, z, c)

    def on_x(k):
        return place((x + k) % NX, y, z, c)

    def on_yl_x(j, k):
        return place((x + k) % NX, yh * NYL + (yl + j) % NYL, z, c)

    def on_z(k):
        return place(x, y, (z + k) % NZ, c)

    barrier = pltpu.get_barrier_semaphore()
    others = [sib, far_sib]
    others += [on_y(k) for k in range(1, NY)]
    others += [on_x(k) for k in range(1, NX)]
    others += [on_z(k) for k in range(1, NZ)]
    others += [on_yl_x(j, k) for j in range(1, NYL) for k in range(1, NX)]
    for other in others:
        pl.semaphore_signal(barrier, inc=1, device_id=other, device_id_type=MESH)

    text_load = pltpu.make_async_copy(text_hbm, text_in, in_s.at[0])
    feat_load = pltpu.make_async_copy(feat_hbm, feat, in_s.at[1])
    w_load = pltpu.make_async_copy(w_hbm, w, in_s.at[2])
    feat_load.start()
    w_load.start()
    text_load.start()

    e = w.shape[1]
    feat_load.wait()
    inputs = feat[...].astype(jnp.float32)
    row_sum = jnp.broadcast_to(jnp.sum(inputs, axis=1, keepdims=True), (128, 128))
    sums[mp] = row_sum.T[:8]
    w_load.wait()
    partial = jnp.dot(feat[...], w[...], preferred_element_type=jnp.float32)
    for h in range(2):
        for b in range(2):
            lo = (h * 2 + b) * 32
            part[b, h, :, :e] = partial[lo : lo + 32]
            part[b, h, :, e:] = row_sum[lo : lo + 32]
    cols[mp] = jnp.sum(w[...].astype(jnp.float32), axis=0, keepdims=True)
    text_load.wait()
    text = text_in[...].astype(jnp.float32)
    own_text = (text * unit_scale(text)).astype(jnp.bfloat16)
    txa[c, HERE, x] = own_text[:16]
    txb[c, x, HERE] = own_text[16:]
    pl.semaphore_wait(barrier, len(others))

    core_copy = remote(part.at[1 - c], part_core, pc_s.at[0], pc_r.at[0], sib)
    mates = [sib, far, far_sib]
    col_copies = [remote(cols.at[mp], cols.at[mp], co_s.at[k], co_r.at[k], to) for k, to in enumerate(mates)]

    own_a = txa.at[c, HERE, x]
    a_x = [remote(own_a, own_a, ax_s.at[k - 1], ax_r.at[k - 1], on_x(k)) for k in range(1, NX)]

    def a_at(r, half):
        return txa.at[c, r] if half is None else txa.at[c, r, pl.ds(half * (NX // 2), NX // 2)]

    def b_at(r, half):
        if half is None:
            return txb.at[c, x, r]
        return txb.at[c, x, r, :, pl.ds(0, 640)] if half == 0 else txb.at[c, x, r, :, pl.ds(640, 512)]

    def b_to_x(lo, count, index):
        block = txb.at[c, x, pl.ds(lo, count)]
        return [
            remote(block, block, bx_s.at[index + k - 1], bx_r.at[index + k - 1], on_x(k)) for k in range(1, NX)
        ]

    def to_sib(block, index):
        return remote(block, block, ts_s.at[index], ts_r.at[index], sib)

    b_z = share(b_at, NZ, on_z, bz_s, bz_r)

    sum_copies = [remote(sums.at[mp], sums.at[mp], su_s.at[k], su_r.at[k], to) for k, to in enumerate(mates)]

    core_copy.wait()
    part[c, 1 - yh] += part_core[1 - yh]
    far_copy = remote(part.at[c, 1 - yh], part_far, pc_s.at[1], pc_r.at[1], far)
    wait_all(a_x)
    a_1 = relay(1, a_at, NZ, on_z, az_s, az_r, None)
    b_on = pass_on(b_at, NZ, on_z, bz_s, bz_r, b_z)
    near(b_z)
    b_x = b_to_x(0, 5, 0)
    a_2 = relay(2, a_at, NZ, on_z, az_s, az_r, a_1)
    wait_all(col_copies)
    col = (cols[0] + cols[1]) + (cols[2] + cols[3])
    far_copy.wait()
    joined = part[c, yh] + part_core[yh] + part_far[...]
    project = joined[:, :e] - (joined[:, e : e + 1] / 1536.0) * col
    inv_norm = unit_scale(project)
    unit_img = project * inv_norm
    unit[...] = unit_img
    img[HERE] = unit_img.astype(jnp.bfloat16)

    def img_at(r, half):
        return img.at[r] if half is None else img.at[r, pl.ds(half * 16, 16)]

    img_one = share(img_at, NY, on_y, im_s, im_r)
    finish(b_z, b_on)
    b_x2 = b_to_x(5, 3, 3)
    a_3 = relay(3, a_at, NZ, on_z, az_s, az_r, a_2)
    img_on = pass_on(img_at, NY, on_y, im_s, im_r, img_one)
    wait_all(sum_copies)
    total = (sums[0] + sums[1]) + (sums[2] + sums[3])
    mean_in = jnp.broadcast_to(total[:1] / 1536.0, (128, 128)).T[:, :1]
    turned = (feat[...].astype(jnp.float32) - mean_in).T.astype(jnp.bfloat16)
    for g in range(NYL):
        nt_send[g] = turned[g * 96 : (g + 1) * 96]
    nt[yl] = nt_send[yl]
    to_core = [to_sib(txa.at[c, pl.ds(0, 5)], 0)]
    a_4 = relay(4, a_at, NZ, on_z, az_s, az_r, a_3)
    wait_all(b_x)
    to_core += [to_sib(txb.at[c, :, pl.ds(0, 5)], 1)]
    a_3[1, 0].wait_recv()
    a_3[0, 1].wait_recv()
    to_core += [to_sib(txa.at[c, 5], 2), to_sib(txa.at[c, 7], 4)]
    near(img_one)
    finish(img_one, img_on)
    wait_all(b_x2)
    to_core += [to_sib(txb.at[c, :, pl.ds(5, 3)], 3)]
    for copies in (a_1, a_2, a_3, a_4):
        for copy in copies.values():
            copy.wait_send()
    for copy in a_4.values():
        copy.wait_recv()
    to_core += [to_sib(txa.at[c, 6], 5)]
    nt_copies = [
        remote(nt_send.at[(yl + k) % NYL], nt.at[yl], nt_s.at[k - 1], nt_r.at[k - 1], on_yl(k))
        for k in range(1, NYL)
    ]

    def add_texts(block, first):
        texts = block[...].reshape(NX * NZ * 16, -1)
        images = img[...].reshape(NY * 32, -1)
        score = lax.dot_general(images, texts, NT, preferred_element_type=jnp.float32)
        slope = jax.nn.sigmoid(logit_scale * score + logit_bias).astype(jnp.bfloat16)
        terms = jnp.dot(slope, texts, preferred_element_type=jnp.float32).reshape(grad.shape)
        grad[...] = terms if first else grad[...] + terms

    add_texts(txa.at[c], True)
    add_texts(txb.at[c], False)
    wait_all(to_core)
    add_texts(txa.at[1 - c], False)
    add_texts(txb.at[1 - c], False)

    for r in (5, 7, 6, 3, 1):
        gs[r] = grad[r].astype(jnp.bfloat16)

    def give(src, dst, index, k):
        return remote(src, dst, gy_s.at[index], gy_r.at[index], on_y(k))

    three = [give(gs.at[5], g_three.at[0], 0, 1), give(gs.at[7], g_three.at[1], 1, NY - 1)]
    four = [
        give(gs.at[6, pl.ds(0, 16)], g_four.at[0], 2, 2),
        give(gs.at[6, pl.ds(16, 16)], g_four.at[1], 3, NY - 2),
    ]
    one = [give(gs.at[3], g_one.at[0], 4, 1), give(gs.at[1], g_one.at[1], 5, NY - 1)]
    own_b16 = img[HERE].astype(jnp.float32)
    own_t = jnp.concatenate([txa[c, HERE, x], txb[c, x, HERE]], axis=0).astype(jnp.float32)
    own_logit = logit_scale * jnp.sum(own_b16 * own_t, axis=1, keepdims=True) + logit_bias
    wrong = jax.nn.sigmoid(own_logit).astype(jnp.bfloat16).astype(jnp.float32)
    right = (-jax.nn.sigmoid(-own_logit)).astype(jnp.bfloat16).astype(jnp.float32)
    grad_unit = grad[HERE] + (right - wrong) * own_t
    wsend[...] = jnp.zeros_like(wsend)
    two = []
    for side, k in ((0, 2), (1, NY - 2)):
        three[side].wait()
        four[side].wait()
        far_sum = grad[(HERE + k) % NY] + g_three[side].astype(jnp.float32)
        lo, hi = far_sum[:16], far_sum[16:]
        if side == 0:
            lo = lo + g_four[0].astype(jnp.float32)
        else:
            hi = hi + g_four[1].astype(jnp.float32)
        g_sum[side, :16] = lo.astype(jnp.bfloat16)
        g_sum[side, 16:] = hi.astype(jnp.bfloat16)
        two.append(give(g_sum.at[side], g_two.at[side], 6 + side, k))
    wait_all(one + two)
    for side in range(2):
        grad_unit = grad_unit + g_one[side].astype(jnp.float32) + g_two[side].astype(jnp.float32)
    grad_unit = logit_scale * grad_unit
    unit_img = unit[...]
    along = jnp.sum(unit_img * grad_unit, axis=1, keepdims=True)
    gproj[c, HERE] = (inv_norm * (grad_unit - unit_img * along)).astype(jnp.bfloat16)

    def gp_at(r, half):
        return gproj.at[c, r] if half is None else gproj.at[c, r, pl.ds(half * 16, 16)]

    def gp_to_sib(lo, count, index):
        block = gproj.at[c, pl.ds(lo, count)]
        return remote(block, block, gc_s.at[index], gc_r.at[index], sib)

    gp_one = share(gp_at, NY, on_y, gp_s, gp_r)
    wait_all(nt_copies)
    gp_on = pass_on(gp_at, NY, on_y, gp_s, gp_r, gp_one)
    near(gp_one)
    gp_core = [gp_to_sib(0, 5, 0)]
    finish(gp_one, gp_on)
    gp_core += [gp_to_sib(5, 3, 1)]
    wait_all(gp_core)

    def group_rows(g):
        low, high = (g - y + HERE + NY) % NY, (g - y + HERE + NY + NYL) % NY
        return jnp.concatenate([gproj[0, low], gproj[1, low], gproj[0, high], gproj[1, high]], axis=0)

    weight_part = jnp.dot(nt[0], group_rows(0), preferred_element_type=jnp.float32)
    for g in range(1, NYL):
        weight_part += jnp.dot(nt[g], group_rows(g), preferred_element_type=jnp.float32)
    weight_part = weight_part.astype(jnp.bfloat16)
    slots = tile_slots()
    for i, j, tx, tz, k in slots:
        wsend[tx, tz, k] = weight_part[i * 16 : (i + 1) * 16, j * 128 : (j + 1) * 128]
    wx_copies = [
        remote(wsend.at[(x + k) % NX], wx.at[x], wx_s.at[k - 1], wx_r.at[k - 1], on_x(k)) for k in range(1, NX)
    ]
    wx[x] = wsend[x]
    rows = group_rows(yl)
    grad_normed = lax.dot_general(rows, w[...], NT, preferred_element_type=jnp.float32)
    grad_total = jnp.sum(rows.astype(jnp.float32) * col, axis=1, keepdims=True)
    gfeat_ref[...] = (grad_normed - grad_total / 1536.0).astype(jnp.bfloat16)
    wait_all(wx_copies)
    over_x = wx[0].astype(jnp.float32)
    for k in range(1, NX):
        over_x += wx[k].astype(jnp.float32)
    zsend[...] = over_x.astype(jnp.bfloat16)
    wz_copies = [
        remote(zsend.at[(z + k) % NZ], wz.at[z], wz_s.at[k - 1], wz_r.at[k - 1], on_z(k)) for k in range(1, NZ)
    ]
    wz[z] = zsend[z]
    wait_all(wz_copies)
    over_z = wz[0].astype(jnp.float32)
    for k in range(1, NZ):
        over_z += wz[k].astype(jnp.float32)
    done = over_z.astype(jnp.bfloat16)
    fin_a[HERE, x, yl] = done[0]
    fin_b[x, HERE, yl] = done[1]
    own_fb = fin_b.at[x, HERE, yl]
    fb_y = [remote(own_fb, own_fb, fy_s.at[k - 1], fy_r.at[k - 1], on_yl(k)) for k in range(1, NYL)]
    own_fa = fin_a.at[HERE, x, yl]
    fa_x = [
        remote(own_fa, own_fa, fax_s.at[j * NX + k], fax_r.at[j * NX + k], on_yl_x(j, k))
        for j in range(NYL)
        for k in range(NX)
        if j + k > 0
    ]

    def fa_at(r, half):
        return fin_a.at[r] if half is None else fin_a.at[r, pl.ds(half * (NX // 2), NX // 2)]

    def fb_at(r, half):
        return fin_b.at[x, r] if half is None else fin_b.at[x, r, pl.ds(half * (NYL // 2), NYL // 2)]

    def fb_to_x(lo, count, index):
        block = fin_b.at[x, pl.ds(lo, count)]
        return [
            remote(block, block, fbx_s.at[index + k - 1], fbx_r.at[index + k - 1], on_x(k)) for k in range(1, NX)
        ]

    wait_all(fb_y)
    fb_z = share(fb_at, NZ, on_z, fbz_s, fbz_r)
    wait_all(fa_x)
    fa_z = share(fa_at, NZ, on_z, faz_s, faz_r)
    fb_on = pass_on(fb_at, NZ, on_z, fbz_s, fbz_r, fb_z)
    near(fb_z)
    fb_x = fb_to_x(0, 5, 0)
    fa_on = pass_on(fa_at, NZ, on_z, faz_s, faz_r, fa_z)
    finish(fb_z, fb_on)
    fb_x += fb_to_x(5, 3, 3)
    near(fa_z)
    finish(fa_z, fa_on)
    wait_all(fb_x)
    at_z = [(tz - z + HERE + NZ) % NZ for tz in range(NZ)]
    for g in range(NYL):
        for i, j, tx, tz, k in slots:
            tile = fin_a[at_z[tz], tx, g] if k == 0 else fin_b[tx, at_z[tz], g]
            gweight_ref[g * 96 + i * 16 : g * 96 + (i + 1) * 16, j * 128 : (j + 1) * 128] = tile.astype(jnp.float32)


def shards(features, proj_weight, texts):
    rows, width = features.shape
    e = proj_weight.shape[1]
    bf16, f32 = jnp.bfloat16, jnp.float32
    dma = pltpu.SemaphoreType.DMA
    counts = [3, 16, 6, 8, 6, 3, 3, NYL - 1, 2, 8, 8, 8, 2, NX - 1, NZ - 1, NYL - 1, NYL * NX, 8, 6, 8]
    semaphores = [dma((3,))] + [dma((n,)) for n in counts for _ in range(2)]
    hbm = pl.BlockSpec(memory_space=pltpu.HBM)
    grad_features, grad_weight = pl.pallas_call(
        kernel,
        out_shape=(
            jax.ShapeDtypeStruct((rows, width), bf16),
            jax.ShapeDtypeStruct((width, e), f32),
        ),
        in_specs=[hbm] * 3,
        out_specs=[pl.BlockSpec(memory_space=pltpu.VMEM)] * 2,
        scratch_shapes=[
            pltpu.VMEM((rows, width), bf16),
            pltpu.VMEM((width, e), bf16),
            pltpu.VMEM((32, e), bf16),
            pltpu.VMEM((2, NZ, NX, 16, e), bf16),
            pltpu.VMEM((2, NX, NZ, 16, e), bf16),
            pltpu.VMEM((4, 8, 128), f32),
            pltpu.VMEM((4, 1, e), f32),
            pltpu.VMEM((NYL, width // NYL, rows), bf16),
            pltpu.VMEM((NYL, width // NYL, rows), bf16),
            pltpu.VMEM((2, 2, 32, e + 128), f32),
            pltpu.VMEM((2, 32, e + 128), f32),
            pltpu.VMEM((32, e + 128), f32),
            pltpu.VMEM((32, e), f32),
            pltpu.VMEM((NY, 32, e), bf16),
            pltpu.VMEM((NY, 32, e), f32),
            pltpu.VMEM((NY, 32, e), bf16),
            pltpu.VMEM((2, 32, e), bf16),
            pltpu.VMEM((2, 16, e), bf16),
            pltpu.VMEM((2, 32, e), bf16),
            pltpu.VMEM((2, 32, e), bf16),
            pltpu.VMEM((2, 32, e), bf16),
            pltpu.VMEM((2, NY, 32, e), bf16),
            pltpu.VMEM((NX, NZ, 2, 16, 128), bf16),
            pltpu.VMEM((NX, NZ, 2, 16, 128), bf16),
            pltpu.VMEM((NZ, 2, 16, 128), bf16),
            pltpu.VMEM((NZ, 2, 16, 128), bf16),
            pltpu.VMEM((NZ, NX, NYL, 16, 128), bf16),
            pltpu.VMEM((NX, NZ, NYL, 16, 128), bf16),
        ]
        + semaphores,
        compiler_params=pltpu.CompilerParams(
            collective_id=0, has_side_effects=True, vmem_limit_bytes=60 << 20
        ),
        cost_estimate=pl.CostEstimate(flops=2_750_000_000, bytes_accessed=8_000_000, transcendentals=524288),
        name="head_loss",
    )(features, proj_weight, texts)
    return grad_features, grad_weight


def solution(mesh):
    return jax.shard_map(
        shards,
        mesh=mesh,
        in_specs=(P("dp", "mp"), P("mp", None), P(("dp", "mp"), None)),
        out_specs=(P("dp", "mp"), P("mp", None)),
        check_vma=False,
    )
```
